32 devices in a mesh: group: 2 (over y), ctx: 4 (over z), head: 2 (over x), pool: 2 (over core).
Axes of the slice: x: 2, y: 2, z: 4, core: 2. Of those that a mesh axis runs over, the one named last changes fastest.
Arguments:
- queries: bfloat16 [1024, 8192], P(('group', 'ctx'), ('head', 'pool')), parts along dimension 0, may hold values from -100 to 100
- new_kv: bfloat16 [2, 1024, 1024], P(None, ('group', 'ctx'), ('head', 'pool')), parts along dimension 1, may hold values from -5 to 5
- pool: bfloat16 [2, 64, 128, 1024], P(None, ('group', 'ctx'), None, ('head', 'pool')), parts along dimension 1, may hold values from -4.5 to 4.5
- block_table: int32 [64], P('group'), parts along dimension 0, may hold values from 0 to 31, as said below
- span_order: int32 [8], P('group'), parts along dimension 0, may hold values from 0 to 3, each once
Outputs:
- attended: bfloat16 [1024, 8192], P(('group', 'ctx'), ('head', 'pool')), parts along dimension 0
The draws below stay inside these ranges and needn't reach their ends.
There are 2 independent parts, one for each index of `group`. The reference program is written for one: setup_inputs(seed, part) draws one part's arguments, and reference() takes and returns one part's arrays. A program takes and returns all parts, laid end to end along the dimension named above; each array names one. Nothing has to cross between parts.
Inputs may be any that keep to these rules, and one draw needn't show every extreme that they name: `block_table`: all ids differ. Index h of ctx holds pool ids h * 8 to (h + 1) * 8 - 1. In each aligned group of 8 entries (entries k * 8 to (k + 1) * 8 - 1), every index of ctx holds either none or exactly 2 of the ids.
All inputs are finite; a program needn't handle non-finite values.
Results may differ from the reference program's by a relative error of at most 0.0045.
Values may be sent and summed in bfloat16 or wider, within the bound.
A program may use at most 128 MiB of HBM per device.

```python
import math
import jax
import jax.numpy as jnp
from jax import lax

HD = 128
QH = 64
KVH = 8
BLK = 128
CAP = 2
Q_DEV = 128
PB_DEV = 8
POOL_DEV = 8
NEW = 512
PREFIX_BLOCKS = 32
PREFIX = 4096
POOL_BLOCKS = 32
N_CTX = 4


def draw_pair(key):
    query_key = jax.random.fold_in(key, 101)
    keys_key = jax.random.fold_in(key, 202)
    values_key = jax.random.fold_in(key, 303)
    base_query = jnp.clip(jax.random.normal(query_key, (NEW, QH, HD), jnp.float32), -4.0, 4.0)
    key_rows = jnp.clip(jax.random.normal(keys_key, (NEW, KVH, HD), jnp.float32), -4.4, 4.4)
    value_rows = jnp.clip(jax.random.normal(values_key, (NEW, KVH, HD), jnp.float32), -4.4, 4.4)
    query_rows = 2.5 * base_query
    stacked = jnp.stack([key_rows, value_rows]).reshape(2, NEW, KVH * HD)
    return (query_rows.reshape(NEW, QH * HD), stacked)


def draw_queries(key, part):
    return draw_pair(key)[0].astype(jnp.bfloat16)


def draw_new_kv(key, part):
    return draw_pair(key)[1].astype(jnp.bfloat16)


def draw_block_table(key, part):
    per_owner = PB_DEV // CAP
    hot_bias = jax.random.randint(jax.random.fold_in(key, 7), (N_CTX,), 0, 4) * 256
    noise_score = jax.random.randint(jax.random.fold_in(key, 8), (N_CTX, N_CTX), 0, 256)
    holder_score = (noise_score + hot_bias[None, :]) * N_CTX + jnp.arange(N_CTX, dtype=jnp.int32)[None, :]
    chosen = lax.top_k(holder_score, per_owner)[1].astype(jnp.int32)
    holders = jnp.repeat(chosen, CAP, axis=1)
    within = jnp.tile(jnp.arange(CAP, dtype=jnp.int32), per_owner)
    rotation = jax.random.randint(jax.random.fold_in(key, 9), (N_CTX,), 0, POOL_DEV)
    owners = jnp.arange(N_CTX, dtype=jnp.int32)[:, None]
    pool_slot = (owners * CAP + within[None, :] + rotation[holders]) % POOL_DEV
    block_ids = holders * POOL_DEV + pool_slot
    shuffle_score = jax.random.randint(jax.random.fold_in(key, 10), (N_CTX, PB_DEV), 0, 4096) * PB_DEV + jnp.arange(PB_DEV, dtype=jnp.int32)[None, :]
    shuffle = jnp.argsort(shuffle_score, axis=1, stable=True)
    block_ids = jnp.take_along_axis(block_ids, shuffle, axis=1)
    return block_ids.reshape(-1).astype(jnp.int32)


def block_levels(stream_key, shape, shards, least, top_value):
    factor_of, own = 1.0, jax.random.fold_in(stream_key, 6)
    for axis_at, blocks in shards:
        steps = jnp.exp(jax.random.uniform(jax.random.fold_in(own, axis_at), (blocks,), jnp.float32, least / len(shards), top_value / len(shards)))
        factor_of = factor_of * jnp.repeat(steps, shape[axis_at] // blocks).reshape([-1 if axis == axis_at else 1 for axis in range(len(shape))])
    return factor_of


def scatter_about(stream_key, dims, scale, limit, pieces=(), kind=jnp.bfloat16):
    result = jax.random.normal(stream_key, dims, jnp.float32) * scale
    if len(pieces) > 0:
        result = block_levels(stream_key, dims, pieces, -0.22, 0.18) * result
    return jnp.clip(result, min=-limit, max=limit).astype(kind)


def setup_inputs(seed: int = 0, part: int = 0) -> dict:
    key_of = jax.random.split(jax.random.key(seed), 6)
    part_splits = jax.random.split(jax.random.fold_in(key_of[5], part), 6)
    queries = draw_queries(jax.random.fold_in(jax.random.fold_in(key_of[5], part), 71), part)
    new_kv = draw_new_kv(jax.random.fold_in(jax.random.fold_in(key_of[5], part), 71), part)
    pool = scatter_about(part_splits[2], (2, POOL_BLOCKS, BLK, KVH * HD), 1.0, 4.5, ((1, 4), (3, 4)))
    block_table = draw_block_table(jax.random.fold_in(jax.random.fold_in(key_of[5], part), 71), part)
    span_order = jax.random.permutation(part_splits[4], N_CTX).astype(jnp.int32)
    return {"queries": queries, "new_kv": new_kv, "pool": pool, "block_table": block_table, "span_order": span_order}


masked_score = -1e+30

def reference(queries, new_kv, pool, block_table, span_order):
    blocks = jnp.take(pool, block_table, axis=1)
    prefix_kv = blocks.reshape(2, PREFIX_BLOCKS * BLK, KVH * HD)
    context = jnp.concatenate([prefix_kv, new_kv], axis=1)
    new_index = jnp.arange(NEW, dtype=jnp.int32)
    query_pos = PREFIX + span_order[new_index // Q_DEV] * Q_DEV + new_index % Q_DEV
    key_pos = jnp.concatenate([jnp.arange(PREFIX, dtype=jnp.int32), query_pos.astype(jnp.int32)])
    allowed = key_pos[None, :] <= query_pos[:, None]
    query_heads = queries.reshape(NEW, QH, HD)
    key_heads = context[0].reshape(PREFIX + NEW, KVH, HD)
    value_heads = context[1].reshape(PREFIX + NEW, KVH, HD)
    per_group = QH // KVH
    score_scale = 1.0 / math.sqrt(HD)

    def one_head(head_index):
        query_head = lax.dynamic_index_in_dim(query_heads, head_index, 1, keepdims=False)
        key_head = lax.dynamic_index_in_dim(key_heads, head_index // per_group, 1, keepdims=False)
        value_head = lax.dynamic_index_in_dim(value_heads, head_index // per_group, 1, keepdims=False)
        scores = jnp.dot(query_head, key_head.T, preferred_element_type=jnp.float32) * score_scale
        scores = jnp.where(allowed, scores, masked_score)
        row_max = lax.optimization_barrier(jnp.max(scores, axis=1, keepdims=True))
        exp_scores = jnp.where(allowed, jnp.exp(scores - row_max), 0.0)
        row_total = lax.optimization_barrier(jnp.sum(exp_scores, axis=1, keepdims=True))
        weighted = jnp.dot(exp_scores.astype(jnp.bfloat16), value_head, preferred_element_type=jnp.float32)
        return weighted / row_total
    per_head = lax.map(one_head, jnp.arange(QH, dtype=jnp.int32))
    return per_head.transpose(1, 0, 2).reshape(NEW, QH * HD).astype(jnp.bfloat16)
```

```python
import functools
import math

import jax
import jax.numpy as jnp
from jax import lax
from jax.experimental import pallas as pl
from jax.experimental.pallas import tpu as pltpu
from jax.sharding import PartitionSpec as P

HD = 128
QH = 64
KVH = 8
CAP = 2


masked_score = -1e30


def lookup(indices, table):
    slots = jnp.arange(table.shape[0], dtype=jnp.int32)
    return jnp.sum(jnp.where(indices[:, None] == slots[None, :], table[None, :], 0), axis=1)


def key_positions(row_count, resident_rows, prefix_rows_dev, span_order, queries_dev, prefix_total):
    global_row = jnp.arange(row_count, dtype=jnp.int32)
    owner_index = global_row // resident_rows
    offset = global_row - owner_index * resident_rows
    span_index = lookup(owner_index, span_order)
    from_new = prefix_total + span_index * queries_dev + offset - prefix_rows_dev
    return jnp.where(offset < prefix_rows_dev, owner_index * prefix_rows_dev + offset, from_new)


def attend(state_now, query_rows, query_pos, kv_piece, key_pos, score_scale):
    acc_out, acc_max, acc_sum = state_now
    kv_heads = query_rows.shape[0]
    head_dim = query_rows.shape[2]
    row_count = kv_piece.shape[1]
    key_block = kv_piece[0].reshape(row_count, kv_heads, head_dim)
    value_block = kv_piece[1].reshape(row_count, kv_heads, head_dim)
    scores = (
        lax.dot_general(
            query_rows, key_block, (((2,), (2,)), ((0,), (1,))), preferred_element_type=jnp.float32
        )
        * score_scale
    )
    allowed = key_pos[None, None, :] <= query_pos[None, :, None]
    scores = jnp.where(allowed, scores, masked_score)
    new_max = jnp.maximum(acc_max, jnp.max(scores, axis=2))
    correct = jnp.exp(acc_max - new_max)
    exp_scores = jnp.where(allowed, jnp.exp(scores - new_max[:, :, None]), 0.0)
    new_sum = acc_sum * correct + jnp.sum(exp_scores, axis=2)
    weights = exp_scores.astype(jnp.bfloat16)
    update = lax.dot_general(
        weights, value_block, (((2,), (0,)), ((0,), (1,))), preferred_element_type=jnp.float32
    )
    return (acc_out * correct[:, :, None] + update, new_max, new_sum)


def attend_piece(state_now, query_rows, query_pos, kv_piece, key_pos, score_scale):
    row_count = kv_piece.shape[1]
    block_rows = row_count
    while block_rows > 2048 and block_rows % 2 == 0:
        block_rows = block_rows // 2
    block_count = row_count // block_rows
    blocks = jnp.moveaxis(kv_piece.reshape(2, block_count, block_rows, kv_piece.shape[2]), 1, 0)
    positions = key_pos.reshape(block_count, block_rows)

    def one_block(state_inner, block_item):
        return (
            attend(state_inner, query_rows, query_pos, block_item[0], block_item[1], score_scale),
            None,
        )

    final_state, unused = lax.scan(one_block, state_now, (blocks, positions))
    return final_state


def routed(queries, new_kv, pool, block_table, span_order):
    cycle_size = lax.axis_size("ctx")
    my_index = lax.axis_index("ctx")
    per_group = QH // KVH
    queries_dev = queries.shape[0]
    kv_heads = new_kv.shape[2] // HD
    pool_dev = pool.shape[1]
    block_len = pool.shape[2]
    blocks_dev = block_table.shape[0] // cycle_size
    owner_table = block_table.reshape(cycle_size, blocks_dev)
    holder = owner_table // pool_dev
    local_id = owner_table - holder * pool_dev
    same_holder = holder[:, :, None] == holder[:, None, :]
    earlier = (
        jnp.arange(blocks_dev, dtype=jnp.int32)[:, None]
        < jnp.arange(blocks_dev, dtype=jnp.int32)[None, :]
    )
    rank_in_list = jnp.sum((same_holder & earlier[None, :, :]).astype(jnp.int32), axis=1)
    slot_match = (holder[:, None, :] == my_index) & (
        rank_in_list[:, None, :] == jnp.arange(CAP, dtype=jnp.int32)[None, :, None]
    )
    source = jnp.sum(jnp.where(slot_match, local_id[:, None, :], 0), axis=2)
    filled = jnp.any(slot_match, axis=2)
    picked = jnp.take(pool, source.reshape(-1), axis=1)
    picked = jnp.where(filled.reshape(1, -1, 1, 1), picked, jnp.zeros_like(picked))
    outgoing = picked.reshape(2, cycle_size, CAP, block_len, pool.shape[3])
    incoming = lax.all_to_all(outgoing, "ctx", split_axis=1, concat_axis=1, tiled=True)
    my_holder = lax.dynamic_index_in_dim(holder, my_index, 0, keepdims=False)
    my_rank = lax.dynamic_index_in_dim(rank_in_list, my_index, 0, keepdims=False)
    flat_slot = my_holder * CAP + my_rank
    arrived = incoming.reshape(2, cycle_size * CAP, block_len, pool.shape[3])
    prefix_kv = jnp.take(arrived, flat_slot, axis=1).reshape(
        2, blocks_dev * block_len, pool.shape[3]
    )
    resident = jnp.concatenate([prefix_kv, new_kv], axis=1)
    resident_rows = resident.shape[1]
    prefix_rows_dev = blocks_dev * block_len
    prefix_total = cycle_size * prefix_rows_dev
    score_scale = 1.0 / math.sqrt(HD)
    row_offsets = jnp.arange(queries_dev, dtype=jnp.int32)
    own_span = lookup(my_index[None], span_order)[0]
    own_pos = jnp.repeat(prefix_total + own_span * queries_dev + row_offsets, per_group)
    query_rows = (
        queries.reshape(queries_dev, kv_heads, per_group, HD)
        .transpose(1, 0, 2, 3)
        .reshape(kv_heads, queries_dev * per_group, HD)
    )
    grouped_rows = queries_dev * per_group
    start_state = (
        jnp.zeros((kv_heads, grouped_rows, HD), jnp.float32),
        jnp.full((kv_heads, grouped_rows), masked_score, jnp.float32),
        jnp.zeros((kv_heads, grouped_rows), jnp.float32),
    )
    kv_piece = lax.all_gather(resident, "ctx", axis=1, tiled=True)
    positions = key_positions(
        kv_piece.shape[1], resident_rows, prefix_rows_dev, span_order, queries_dev, prefix_total
    )
    final_state = attend_piece(start_state, query_rows, own_pos, kv_piece, positions, score_scale)
    out_sum, out_max, out_total = final_state
    result = out_sum / out_total[:, :, None]
    result = (
        result.reshape(kv_heads, queries_dev, per_group, HD)
        .transpose(1, 0, 2, 3)
        .reshape(queries_dev, kv_heads * per_group * HD)
    )
    return result.astype(jnp.bfloat16)


def context_kernel(
    n, kv_heads, per_group, splits, offload,
    span_ref, queries_ref, new_ref, pool_ref, out_ref,
    kv, qs, acc, row_max, part_out, part_stat, got_out, got_stat,
    load_sem, query_sem, send_sem, recv_sem, edge_send, edge_recv,
):
    me = lax.axis_index("ctx")
    pool_dev, block_len = pool_ref.shape[1], pool_ref.shape[2]
    pieces, group_blocks = kv.shape[1], kv.shape[3]
    keys = group_blocks * block_len
    rows = queries_ref.shape[0]
    tile_heads = 2 if per_group % 2 == 0 else 1
    tile_rows = tile_heads * rows
    tiles = per_group // tile_heads
    unit = math.log2(math.e) / math.sqrt(HD)

    at_edge = (me == 0) | (me == n - 1)

    loads = [[] for _ in range(pieces)]
    count = 0
    for piece in range(pieces):
        kv_head, split = divmod(piece, splits)
        columns = pl.ds(kv_head * HD, HD)
        first = split * group_blocks
        pool_blocks = min(group_blocks, pool_dev - first)
        for t in range(2):
            if pool_blocks > 0:
                loads[piece].append(
                    pltpu.make_async_copy(
                        pool_ref.at[t, pl.ds(first, pool_blocks), :, columns],
                        kv.at[me, piece, t, pl.ds(0, pool_blocks)],
                        load_sem.at[count],
                    )
                )
                count += 1
            if pool_blocks < group_blocks:
                loads[piece].append(
                    pltpu.make_async_copy(
                        new_ref.at[t, :, columns],
                        kv.at[me, piece, t, group_blocks - 1],
                        load_sem.at[count],
                    )
                )
                count += 1
    for piece in range(pieces):
        for load in loads[piece]:
            load.start()
    query_loads = []
    for head in range(kv_heads * per_group):
        query_loads.append(
            pltpu.make_async_copy(
                queries_ref.at[:, pl.ds(head * HD, HD)],
                qs.at[head // per_group, head % per_group],
                query_sem.at[head],
            )
        )
        query_loads[-1].start()

    barrier = pltpu.get_barrier_semaphore()

    @pl.when(me > 0)
    def _():
        pl.semaphore_signal(
            barrier, inc=1, device_id={"ctx": me - 1}, device_id_type=pl.DeviceIdType.MESH
        )

    @pl.when(me < n - 1)
    def _():
        pl.semaphore_signal(
            barrier, inc=1, device_id={"ctx": me + 1}, device_id_type=pl.DeviceIdType.MESH
        )

    @pl.when(at_edge)
    def _():
        pl.semaphore_wait(barrier, 1)

    @pl.when(jnp.logical_not(at_edge))
    def _():
        pl.semaphore_wait(barrier, 2)

    def piece_copy(source, piece, side):
        return pltpu.make_async_remote_copy(
            src_ref=kv.at[source, piece],
            dst_ref=kv.at[source, piece],
            send_sem=send_sem.at[side, source, piece],
            recv_sem=recv_sem.at[source, piece],
            device_id={"ctx": me + 2 * side - 1},
            device_id_type=pl.DeviceIdType.MESH,
        )

    def edge_copy(index, source, target, device):
        return pltpu.make_async_remote_copy(
            src_ref=source,
            dst_ref=target,
            send_sem=edge_send.at[index],
            recv_sem=edge_recv.at[index],
            device_id={"ctx": device},
            device_id_type=pl.DeviceIdType.MESH,
        )

    by_edge = (me == 1) | (me == n - 2)
    inner = jnp.where(me == 0, 1, n - 2)
    outer = jnp.where(me == 1, 0, n - 1)

    for piece in range(pieces):
        for load in loads[piece]:
            load.wait()

        @pl.when(me > 0)
        def _():
            piece_copy(me, piece, 0).start()

        @pl.when(me < n - 1)
        def _():
            piece_copy(me, piece, 1).start()

        if offload and piece == splits - 1:
            for head in range(per_group):
                query_loads[head].wait()

            @pl.when(at_edge)
            def _():
                edge_copy(0, qs.at[0], qs.at[kv_heads], inner).start()

    for head in range(per_group if offload else 0, kv_heads * per_group):
        query_loads[head].wait()

    acc[...] = jnp.zeros(acc.shape, jnp.float32)
    row_max[...] = jnp.full(row_max.shape, masked_score, jnp.float32)

    query_row = lax.broadcasted_iota(jnp.int32, (tile_heads, rows, block_len), 1).reshape(
        tile_rows, block_len
    )
    key_column = lax.broadcasted_iota(jnp.int32, (tile_rows, block_len), 1)
    offset = key_column - query_row

    def attend_tiles(group, source, piece, asker):
        key_rows = kv[source, piece, 0].reshape(keys, HD)
        value_rows = kv[source, piece, 1].reshape(keys, HD)
        value_ones = jnp.concatenate([value_rows, jnp.ones_like(value_rows)], axis=1)
        has_new = lax.rem(piece, splits) == splits - 1
        limit = (span_ref[asker] - span_ref[source]) * rows
        limit = jnp.where(has_new, limit, rows + block_len)
        allowed = offset <= limit
        for tile in range(tiles):
            heads = pl.ds(tile * tile_heads, tile_heads)
            query_tile = qs[group, heads].reshape(tile_rows, HD)
            scores = lax.dot_general(
                query_tile, key_rows, (((1,), (1,)), ((), ())), preferred_element_type=jnp.float32
            )
            last = jnp.where(allowed, scores[:, keys - block_len :], masked_score)
            scores = jnp.concatenate([scores[:, : keys - block_len], last], axis=1)
            span = pl.ds(tile * tile_rows, tile_rows)
            old_max = row_max[group, span]
            new_max = jnp.maximum(old_max, jnp.max(scores, axis=1, keepdims=True))
            row_max[group, span] = new_max
            correct = jnp.exp2((old_max - new_max) * unit)
            wide = jnp.concatenate([new_max] * group_blocks, axis=1)
            weights = jnp.exp2((scores - wide) * unit).astype(jnp.bfloat16)
            update = jnp.dot(weights, value_ones, preferred_element_type=jnp.float32)
            acc[group, span] = (
                acc[group, span] * jnp.concatenate([correct, correct], axis=1) + update
            )

    def own_piece(piece, carry):
        attend_tiles(piece // splits, me, piece, me)
        return carry

    lax.fori_loop(0, pieces, own_piece, 0)

    if offload:

        @pl.when(by_edge)
        def _():
            edge_copy(0, qs.at[0], qs.at[kv_heads], outer).wait_recv()

    diagonal = lax.broadcasted_iota(jnp.int32, (rows, HD), 0) == lax.broadcasted_iota(
        jnp.int32, (rows, HD), 1
    )

    def return_part():
        for head in range(per_group):
            span = pl.ds(head * rows, rows)
            total = acc[kv_heads, span, HD:]
            part_out[head] = (acc[kv_heads, span, :HD] / total).astype(jnp.bfloat16)
            peak = row_max[kv_heads, span]
            part_stat[0, pl.ds(head, 1)] = jnp.sum(
                jnp.where(diagonal, peak, 0.0), axis=0, keepdims=True
            )
            part_stat[1, pl.ds(head, 1)] = jnp.sum(
                jnp.where(diagonal, total, 0.0), axis=0, keepdims=True
            )
        edge_copy(1, part_out, got_out, outer).start()
        edge_copy(2, part_stat, got_stat, outer).start()

    def arrival(step, carry):
        distance = 1 + step // (2 * pieces)
        piece = (step % (2 * pieces)) // 2
        side = step % 2
        source = me + (1 - 2 * side) * distance
        onward = me + 2 * side - 1
        valid = (source >= 0) & (source < n)
        has_next = (onward >= 0) & (onward < n)
        if offload:
            head_off = piece < splits
            valid = valid & jnp.logical_not(at_edge & head_off & (distance >= 2))
            handed = has_next & head_off & ((onward == 0) | (onward == n - 1))
        else:
            handed = False

        @pl.when(valid)
        def _():
            copy = piece_copy(source, piece, side)
            copy.wait_recv()

            @pl.when(has_next & jnp.logical_not(handed))
            def _():
                copy.start()

            if offload:

                @pl.when(handed)
                def _():
                    attend_tiles(kv_heads, source, piece, onward)

                    @pl.when((distance == n - 2) & (piece == splits - 1))
                    def _():
                        return_part()

            attend_tiles(piece // splits, source, piece, me)

        return carry

    lax.fori_loop(0, 2 * pieces * (n - 1), arrival, 0)

    def settle(group, head):
        columns = pl.ds((group * per_group + head) * HD, HD)
        span = pl.ds(head * rows, rows)
        out_ref[:, columns] = (acc[group, span, :HD] / acc[group, span, HD:]).astype(out_ref.dtype)

    def settle_with_part(head):
        span = pl.ds(head * rows, rows)
        their_max = jnp.broadcast_to(got_stat[0, pl.ds(head, 1)], (HD, rows)).T
        their_total = jnp.broadcast_to(got_stat[1, pl.ds(head, 1)], (HD, rows)).T
        my_max = row_max[0, span]
        top = jnp.maximum(my_max, their_max)
        mine = jnp.exp2((my_max - top) * unit)
        theirs = jnp.exp2((their_max - top) * unit) * their_total
        total = acc[0, span, HD:] * mine + theirs
        summed = acc[0, span, :HD] * mine + got_out[head].astype(jnp.float32) * theirs
        out_ref[:, pl.ds(head * HD, HD)] = (summed / total).astype(out_ref.dtype)

    for group in range(1 if offload else 0, kv_heads):
        for head in range(per_group):
            settle(group, head)
    if offload:

        @pl.when(at_edge)
        def _():
            edge_copy(1, part_out, got_out, inner).wait_recv()
            edge_copy(2, part_stat, got_stat, inner).wait_recv()
            for head in range(per_group):
                settle_with_part(head)

        @pl.when(jnp.logical_not(at_edge))
        def _():
            for head in range(per_group):
                settle(0, head)

    def sent(step, carry):
        distance = step // (2 * pieces)
        piece = (step % (2 * pieces)) // 2
        side = step % 2
        source = me + (1 - 2 * side) * distance
        onward = me + 2 * side - 1
        went = (source >= 0) & (source < n) & (onward >= 0) & (onward < n)
        if offload:
            went = went & jnp.logical_not(
                (distance >= 1) & (piece < splits) & ((onward == 0) | (onward == n - 1))
            )

        @pl.when(went)
        def _():
            piece_copy(source, piece, side).wait_send()

        return carry

    lax.fori_loop(0, 2 * pieces * n, sent, 0)
    if offload:

        @pl.when(at_edge)
        def _():
            edge_copy(0, qs.at[0], qs.at[kv_heads], inner).wait_send()

        @pl.when(by_edge)
        def _():
            edge_copy(1, part_out, got_out, outer).wait_send()
            edge_copy(2, part_stat, got_stat, outer).wait_send()


def local(queries, new_kv, pool, block_table, span_order):
    n = lax.axis_size("ctx")
    pool_dev, block_len = pool.shape[1], pool.shape[2]
    rows = queries.shape[0]
    kv_heads = new_kv.shape[2] // HD
    per_group = QH // KVH
    whole_pool = block_table.shape[0] == n * pool_dev
    if not whole_pool or n < 2 or rows != block_len or rows != HD:
        return routed(queries, new_kv, pool, block_table, span_order)
    blocks = pool_dev + 1
    splits = 3 if blocks % 3 == 0 and blocks > 3 else 1
    pieces = kv_heads * splits
    group_blocks = blocks // splits
    offload = n >= 4 and kv_heads >= 2
    groups = kv_heads + 1 if offload else kv_heads
    group_rows = per_group * rows
    work = queries.shape[1] * rows * block_len * blocks * n
    return pl.pallas_call(
        functools.partial(context_kernel, n, kv_heads, per_group, splits, offload),
        out_shape=jax.ShapeDtypeStruct(queries.shape, jnp.bfloat16),
        in_specs=[
            pl.BlockSpec(memory_space=pltpu.SMEM),
            pl.BlockSpec(memory_space=pl.ANY),
            pl.BlockSpec(memory_space=pl.ANY),
            pl.BlockSpec(memory_space=pl.ANY),
        ],
        out_specs=pl.BlockSpec(memory_space=pltpu.VMEM),
        scratch_shapes=[
            pltpu.VMEM((n, pieces, 2, group_blocks, block_len, HD), jnp.bfloat16),
            pltpu.VMEM((groups, per_group, rows, HD), jnp.bfloat16),
            pltpu.VMEM((groups, group_rows, 2 * HD), jnp.float32),
            pltpu.VMEM((groups, group_rows, HD), jnp.float32),
            pltpu.VMEM((per_group, rows, HD), jnp.bfloat16),
            pltpu.VMEM((2, per_group, HD), jnp.float32),
            pltpu.VMEM((per_group, rows, HD), jnp.bfloat16),
            pltpu.VMEM((2, per_group, HD), jnp.float32),
            pltpu.SemaphoreType.DMA((4 * pieces,)),
            pltpu.SemaphoreType.DMA((kv_heads * per_group,)),
            pltpu.SemaphoreType.DMA((2, n, pieces)),
            pltpu.SemaphoreType.DMA((n, pieces)),
            pltpu.SemaphoreType.DMA((3,)),
            pltpu.SemaphoreType.DMA((3,)),
        ],
        compiler_params=pltpu.CompilerParams(
            collective_id=0, has_side_effects=True, vmem_limit_bytes=40 * 1024 * 1024
        ),
        cost_estimate=pl.CostEstimate(
            flops=4 * work, bytes_accessed=4 * queries.size, transcendentals=work // HD
        ),
        name="context_attention",
    )(span_order, queries, new_kv, pool)


def solution(mesh):
    return jax.shard_map(
        local,
        mesh=mesh,
        in_specs=(
            P(("group", "ctx"), ("head", "pool")),
            P(None, ("group", "ctx"), ("head", "pool")),
            P(None, ("group", "ctx"), None, ("head", "pool")),
            P("group"),
            P("group"),
        ),
        out_specs=P(("group", "ctx"), ("head", "pool")),
        check_vma=False,
    )
```

```python
import functools
import math

import jax
import jax.numpy as jnp
from jax import lax
from jax.experimental import pallas as pl
from jax.experimental.pallas import tpu as pltpu
from jax.sharding import PartitionSpec as P

HD = 128
QH = 64
KVH = 8
CAP = 2


masked_score = -1e30


def lookup(indices, table):
    slots = jnp.arange(table.shape[0], dtype=jnp.int32)
    return jnp.sum(jnp.where(indices[:, None] == slots[None, :], table[None, :], 0), axis=1)


def key_positions(row_count, resident_rows, prefix_rows_dev, span_order, queries_dev, prefix_total):
    global_row = jnp.arange(row_count, dtype=jnp.int32)
    owner_index = global_row // resident_rows
    offset = global_row - owner_index * resident_rows
    span_index = lookup(owner_index, span_order)
    from_new = prefix_total + span_index * queries_dev + offset - prefix_rows_dev
    return jnp.where(offset < prefix_rows_dev, owner_index * prefix_rows_dev + offset, from_new)


def attend(state_now, query_rows, query_pos, kv_piece, key_pos, score_scale):
    acc_out, acc_max, acc_sum = state_now
    kv_heads = query_rows.shape[0]
    head_dim = query_rows.shape[2]
    row_count = kv_piece.shape[1]
    key_block = kv_piece[0].reshape(row_count, kv_heads, head_dim)
    value_block = kv_piece[1].reshape(row_count, kv_heads, head_dim)
    scores = (
        lax.dot_general(
            query_rows, key_block, (((2,), (2,)), ((0,), (1,))), preferred_element_type=jnp.float32
        )
        * score_scale
    )
    allowed = key_pos[None, None, :] <= query_pos[None, :, None]
    scores = jnp.where(allowed, scores, masked_score)
    new_max = jnp.maximum(acc_max, jnp.max(scores, axis=2))
    correct = jnp.exp(acc_max - new_max)
    exp_scores = jnp.where(allowed, jnp.exp(scores - new_max[:, :, None]), 0.0)
    new_sum = acc_sum * correct + jnp.sum(exp_scores, axis=2)
    weights = exp_scores.astype(jnp.bfloat16)
    update = lax.dot_general(
        weights, value_block, (((2,), (0,)), ((0,), (1,))), preferred_element_type=jnp.float32
    )
    return (acc_out * correct[:, :, None] + update, new_max, new_sum)


def attend_piece(state_now, query_rows, query_pos, kv_piece, key_pos, score_scale):
    row_count = kv_piece.shape[1]
    block_rows = row_count
    while block_rows > 2048 and block_rows % 2 == 0:
        block_rows = block_rows // 2
    block_count = row_count // block_rows
    blocks = jnp.moveaxis(kv_piece.reshape(2, block_count, block_rows, kv_piece.shape[2]), 1, 0)
    positions = key_pos.reshape(block_count, block_rows)

    def one_block(state_inner, block_item):
        return (
            attend(state_inner, query_rows, query_pos, block_item[0], block_item[1], score_scale),
            None,
        )

    final_state, unused = lax.scan(one_block, state_now, (blocks, positions))
    return final_state


def routed(queries, new_kv, pool, block_table, span_order):
    cycle_size = lax.axis_size("ctx")
    my_index = lax.axis_index("ctx")
    per_group = QH // KVH
    queries_dev = queries.shape[0]
    kv_heads = new_kv.shape[2] // HD
    pool_dev = pool.shape[1]
    block_len = pool.shape[2]
    blocks_dev = block_table.shape[0] // cycle_size
    owner_table = block_table.reshape(cycle_size, blocks_dev)
    holder = owner_table // pool_dev
    local_id = owner_table - holder * pool_dev
    same_holder = holder[:, :, None] == holder[:, None, :]
    earlier = (
        jnp.arange(blocks_dev, dtype=jnp.int32)[:, None]
        < jnp.arange(blocks_dev, dtype=jnp.int32)[None, :]
    )
    rank_in_list = jnp.sum((same_holder & earlier[None, :, :]).astype(jnp.int32), axis=1)
    slot_match = (holder[:, None, :] == my_index) & (
        rank_in_list[:, None, :] == jnp.arange(CAP, dtype=jnp.int32)[None, :, None]
    )
    source = jnp.sum(jnp.where(slot_match, local_id[:, None, :], 0), axis=2)
    filled = jnp.any(slot_match, axis=2)
    picked = jnp.take(pool, source.reshape(-1), axis=1)
    picked = jnp.where(filled.reshape(1, -1, 1, 1), picked, jnp.zeros_like(picked))
    outgoing = picked.reshape(2, cycle_size, CAP, block_len, pool.shape[3])
    incoming = lax.all_to_all(outgoing, "ctx", split_axis=1, concat_axis=1, tiled=True)
    my_holder = lax.dynamic_index_in_dim(holder, my_index, 0, keepdims=False)
    my_rank = lax.dynamic_index_in_dim(rank_in_list, my_index, 0, keepdims=False)
    flat_slot = my_holder * CAP + my_rank
    arrived = incoming.reshape(2, cycle_size * CAP, block_len, pool.shape[3])
    prefix_kv = jnp.take(arrived, flat_slot, axis=1).reshape(
        2, blocks_dev * block_len, pool.shape[3]
    )
    resident = jnp.concatenate([prefix_kv, new_kv], axis=1)
    resident_rows = resident.shape[1]
    prefix_rows_dev = blocks_dev * block_len
    prefix_total = cycle_size * prefix_rows_dev
    score_scale = 1.0 / math.sqrt(HD)
    row_offsets = jnp.arange(queries_dev, dtype=jnp.int32)
    own_span = lookup(my_index[None], span_order)[0]
    own_pos = jnp.repeat(prefix_total + own_span * queries_dev + row_offsets, per_group)
    query_rows = (
        queries.reshape(queries_dev, kv_heads, per_group, HD)
        .transpose(1, 0, 2, 3)
        .reshape(kv_heads, queries_dev * per_group, HD)
    )
    grouped_rows = queries_dev * per_group
    start_state = (
        jnp.zeros((kv_heads, grouped_rows, HD), jnp.float32),
        jnp.full((kv_heads, grouped_rows), masked_score, jnp.float32),
        jnp.zeros((kv_heads, grouped_rows), jnp.float32),
    )
    kv_piece = lax.all_gather(resident, "ctx", axis=1, tiled=True)
    positions = key_positions(
        kv_piece.shape[1], resident_rows, prefix_rows_dev, span_order, queries_dev, prefix_total
    )
    final_state = attend_piece(start_state, query_rows, own_pos, kv_piece, positions, score_scale)
    out_sum, out_max, out_total = final_state
    result = out_sum / out_total[:, :, None]
    result = (
        result.reshape(kv_heads, queries_dev, per_group, HD)
        .transpose(1, 0, 2, 3)
        .reshape(queries_dev, kv_heads * per_group * HD)
    )
    return result.astype(jnp.bfloat16)


def context_kernel(
    n, kv_heads, per_group, splits, offload,
    span_ref, queries_ref, new_ref, pool_ref, out_ref,
    kv, qs, acc, row_max, part_out, part_stat, got_out, got_stat,
    load_sem, query_sem, send_sem, recv_sem, edge_send, edge_recv,
):
    me = lax.axis_index("ctx")
    pool_dev, block_len = pool_ref.shape[1], pool_ref.shape[2]
    pieces, group_blocks = kv.shape[1], kv.shape[3]
    keys = group_blocks * block_len
    rows = queries_ref.shape[0]
    tile_heads = 2 if per_group % 2 == 0 else 1
    tile_rows = tile_heads * rows
    tiles = per_group // tile_heads
    unit = math.log2(math.e) / math.sqrt(HD)

    at_edge = (me == 0) | (me == n - 1)

    loads = [[] for _ in range(pieces)]
    count = 0
    for piece in range(pieces):
        kv_head, split = divmod(piece, splits)
        columns = pl.ds(kv_head * HD, HD)
        first = split * group_blocks
        pool_blocks = min(group_blocks, pool_dev - first)
        for t in range(2):
            if pool_blocks > 0:
                loads[piece].append(
                    pltpu.make_async_copy(
                        pool_ref.at[t, pl.ds(first, pool_blocks), :, columns],
                        kv.at[me, piece, t, pl.ds(0, pool_blocks)],
                        load_sem.at[count],
                    )
                )
                count += 1
            if pool_blocks < group_blocks:
                loads[piece].append(
                    pltpu.make_async_copy(
                        new_ref.at[t, :, columns],
                        kv.at[me, piece, t, group_blocks - 1],
                        load_sem.at[count],
                    )
                )
                count += 1
    for piece in range(pieces):
        for load in loads[piece]:
            load.start()
    query_loads = []
    for head in range(kv_heads * per_group):
        query_loads.append(
            pltpu.make_async_copy(
                queries_ref.at[:, pl.ds(head * HD, HD)],
                qs.at[head // per_group, head % per_group],
                query_sem.at[head],
            )
        )
        query_loads[-1].start()

    barrier = pltpu.get_barrier_semaphore()

    @pl.when(me > 0)
    def _():
        pl.semaphore_signal(
            barrier, inc=1, device_id={"ctx": me - 1}, device_id_type=pl.DeviceIdType.MESH
        )

    @pl.when(me < n - 1)
    def _():
        pl.semaphore_signal(
            barrier, inc=1, device_id={"ctx": me + 1}, device_id_type=pl.DeviceIdType.MESH
        )

    @pl.when(at_edge)
    def _():
        pl.semaphore_wait(barrier, 1)

    @pl.when(jnp.logical_not(at_edge))
    def _():
        pl.semaphore_wait(barrier, 2)

    def piece_copy(source, piece, side):
        return pltpu.make_async_remote_copy(
            src_ref=kv.at[source, piece],
            dst_ref=kv.at[source, piece],
            send_sem=send_sem.at[side, source, piece],
            recv_sem=recv_sem.at[source, piece],
            device_id={"ctx": me + 2 * side - 1},
            device_id_type=pl.DeviceIdType.MESH,
        )

    def edge_copy(index, source, target, device):
        return pltpu.make_async_remote_copy(
            src_ref=source,
            dst_ref=target,
            send_sem=edge_send.at[index],
            recv_sem=edge_recv.at[index],
            device_id={"ctx": device},
            device_id_type=pl.DeviceIdType.MESH,
        )

    by_edge = (me == 1) | (me == n - 2)
    inner = jnp.where(me == 0, 1, n - 2)
    outer = jnp.where(me == 1, 0, n - 1)

    for piece in range(pieces):
        for load in loads[piece]:
            load.wait()

        @pl.when(me > 0)
        def _():
            piece_copy(me, piece, 0).start()

        @pl.when(me < n - 1)
        def _():
            piece_copy(me, piece, 1).start()

        if offload and piece == splits - 1:
            for head in range(per_group):
                query_loads[head].wait()

            @pl.when(at_edge)
            def _():
                edge_copy(0, qs.at[0], qs.at[kv_heads], inner).start()

    for head in range(per_group if offload else 0, kv_heads * per_group):
        query_loads[head].wait()

    if offload:
        acc[kv_heads] = jnp.zeros(acc.shape[1:], jnp.float32)
        row_max[kv_heads] = jnp.full(row_max.shape[1:], masked_score, jnp.float32)

    query_row = lax.broadcasted_iota(jnp.int32, (tile_heads, rows, block_len), 1).reshape(
        tile_rows, block_len
    )
    key_column = lax.broadcasted_iota(jnp.int32, (tile_rows, block_len), 1)
    offset = key_column - query_row

    def attend_tiles(group, source, piece, count, asker, fresh=False):
        taken = pl.ds(piece, count)
        width = count * keys
        key_rows = kv[source, taken, 0].reshape(width, HD)
        value_rows = kv[source, taken, 1].reshape(width, HD)
        value_ones = jnp.concatenate([value_rows, jnp.ones_like(value_rows)], axis=1)
        limit = (span_ref[asker] - span_ref[source]) * rows
        if count < splits:
            has_new = lax.rem(piece, splits) == splits - 1
            limit = jnp.where(has_new, limit, rows + block_len)
        allowed = offset <= limit
        for tile in range(tiles):
            heads = pl.ds(tile * tile_heads, tile_heads)
            query_tile = qs[group, heads].reshape(tile_rows, HD)
            scores = lax.dot_general(
                query_tile, key_rows, (((1,), (1,)), ((), ())), preferred_element_type=jnp.float32
            )
            last = jnp.where(allowed, scores[:, width - block_len :], masked_score)
            scores = jnp.concatenate([scores[:, : width - block_len], last], axis=1)
            span = pl.ds(tile * tile_rows, tile_rows)
            new_max = jnp.max(scores, axis=1, keepdims=True)
            if fresh:
                new_max = jnp.broadcast_to(new_max, (tile_rows, HD))
            else:
                old_max = row_max[group, span]
                new_max = jnp.maximum(old_max, new_max)
            row_max[group, span] = new_max
            wide = jnp.concatenate([new_max] * (width // HD), axis=1)
            weights = jnp.exp2((scores - wide) * unit).astype(jnp.bfloat16)
            update = jnp.dot(weights, value_ones, preferred_element_type=jnp.float32)
            if not fresh:
                correct = jnp.exp2((old_max - new_max) * unit)
                update += acc[group, span] * jnp.concatenate([correct, correct], axis=1)
            acc[group, span] = update

    def own_head(head, carry):
        attend_tiles(head, me, head * splits, splits, me, fresh=True)
        return carry

    lax.fori_loop(0, kv_heads, own_head, 0)

    if offload:

        @pl.when(by_edge)
        def _():
            edge_copy(0, qs.at[0], qs.at[kv_heads], outer).wait_recv()

    diagonal = lax.broadcasted_iota(jnp.int32, (rows, HD), 0) == lax.broadcasted_iota(
        jnp.int32, (rows, HD), 1
    )

    def return_part():
        for head in range(per_group):
            span = pl.ds(head * rows, rows)
            total = acc[kv_heads, span, HD:]
            part_out[head] = (acc[kv_heads, span, :HD] / total).astype(jnp.bfloat16)
            peak = row_max[kv_heads, span]
            part_stat[0, pl.ds(head, 1)] = jnp.sum(
                jnp.where(diagonal, peak, 0.0), axis=0, keepdims=True
            )
            part_stat[1, pl.ds(head, 1)] = jnp.sum(
                jnp.where(diagonal, total, 0.0), axis=0, keepdims=True
            )
        edge_copy(1, part_out, got_out, outer).start()
        edge_copy(2, part_stat, got_stat, outer).start()

    def arrival(step, carry):
        distance = 1 + step // kv_heads
        head = step % kv_heads

        def about(side):
            source = me + (1 - 2 * side) * distance
            onward = me + 2 * side - 1
            valid = (source >= 0) & (source < n)
            has_next = (onward >= 0) & (onward < n)
            late = (distance >= 2) & (head == kv_heads - 1) & ((source == 0) | (source == n - 1))
            handed = False
            if offload:
                valid = valid & jnp.logical_not(at_edge & (head == 0) & (distance >= 2))
                handed = has_next & (head == 0) & ((onward == 0) | (onward == n - 1))
            return source, onward, valid, late, has_next & jnp.logical_not(handed), handed

        def pass_on(piece, side, source, forward):
            copy = piece_copy(source, piece, side)
            copy.wait_recv()

            @pl.when(forward)
            def _():
                copy.start()

        def one_split(split, carry):
            for side in range(2):
                source, _, valid, late, forward, _ = about(side)

                @pl.when(valid & jnp.logical_not(late))
                def _():
                    pass_on(head * splits + split, side, source, forward)

            return carry

        lax.fori_loop(0, splits, one_split, 0)

        def one_side(side, carry):
            source, onward, valid, late, forward, handed = about(side)

            @pl.when(valid & jnp.logical_not(late))
            def _():
                if offload:

                    @pl.when(handed)
                    def _():
                        attend_tiles(kv_heads, source, head * splits, splits, onward)

                        @pl.when(distance == n - 2)
                        def _():
                            return_part()

                attend_tiles(head, source, head * splits, splits, me)

            @pl.when(valid & late)
            def _():
                def one_late(split, carry):
                    piece = head * splits + split
                    pass_on(piece, side, source, forward)
                    attend_tiles(head, source, piece, 1, me)
                    return carry

                lax.fori_loop(0, splits, one_late, 0)

            return carry

        lax.fori_loop(0, 2, one_side, 0)
        return carry

    lax.fori_loop(0, kv_heads * (n - 1), arrival, 0)

    def settle(group, head):
        columns = pl.ds((group * per_group + head) * HD, HD)
        span = pl.ds(head * rows, rows)
        out_ref[:, columns] = (acc[group, span, :HD] / acc[group, span, HD:]).astype(out_ref.dtype)

    def settle_with_part(head):
        span = pl.ds(head * rows, rows)
        their_max = jnp.broadcast_to(got_stat[0, pl.ds(head, 1)], (HD, rows)).T
        their_total = jnp.broadcast_to(got_stat[1, pl.ds(head, 1)], (HD, rows)).T
        my_max = row_max[0, span]
        top = jnp.maximum(my_max, their_max)
        mine = jnp.exp2((my_max - top) * unit)
        theirs = jnp.exp2((their_max - top) * unit) * their_total
        total = acc[0, span, HD:] * mine + theirs
        summed = acc[0, span, :HD] * mine + got_out[head].astype(jnp.float32) * theirs
        out_ref[:, pl.ds(head * HD, HD)] = (summed / total).astype(out_ref.dtype)

    for group in range(1 if offload else 0, kv_heads):
        for head in range(per_group):
            settle(group, head)
    if offload:

        @pl.when(at_edge)
        def _():
            edge_copy(1, part_out, got_out, inner).wait_recv()
            edge_copy(2, part_stat, got_stat, inner).wait_recv()
            for head in range(per_group):
                settle_with_part(head)

        @pl.when(jnp.logical_not(at_edge))
        def _():
            for head in range(per_group):
                settle(0, head)

    def sent(step, carry):
        distance = step // (2 * pieces)
        piece = (step % (2 * pieces)) // 2
        side = step % 2
        source = me + (1 - 2 * side) * distance
        onward = me + 2 * side - 1
        went = (source >= 0) & (source < n) & (onward >= 0) & (onward < n)
        if offload:
            went = went & jnp.logical_not(
                (distance >= 1) & (piece < splits) & ((onward == 0) | (onward == n - 1))
            )

        @pl.when(went)
        def _():
            piece_copy(source, piece, side).wait_send()

        return carry

    lax.fori_loop(0, 2 * pieces * n, sent, 0)
    if offload:

        @pl.when(at_edge)
        def _():
            edge_copy(0, qs.at[0], qs.at[kv_heads], inner).wait_send()

        @pl.when(by_edge)
        def _():
            edge_copy(1, part_out, got_out, outer).wait_send()
            edge_copy(2, part_stat, got_stat, outer).wait_send()


def local(queries, new_kv, pool, block_table, span_order):
    n = lax.axis_size("ctx")
    pool_dev, block_len = pool.shape[1], pool.shape[2]
    rows = queries.shape[0]
    kv_heads = new_kv.shape[2] // HD
    per_group = QH // KVH
    whole_pool = block_table.shape[0] == n * pool_dev
    if not whole_pool or n < 2 or rows != block_len or rows != HD:
        return routed(queries, new_kv, pool, block_table, span_order)
    blocks = pool_dev + 1
    splits = 3 if blocks % 3 == 0 and blocks > 3 else 1
    pieces = kv_heads * splits
    group_blocks = blocks // splits
    offload = n >= 4 and kv_heads >= 2
    groups = kv_heads + 1 if offload else kv_heads
    group_rows = per_group * rows
    work = queries.shape[1] * rows * block_len * blocks * n
    return pl.pallas_call(
        functools.partial(context_kernel, n, kv_heads, per_group, splits, offload),
        out_shape=jax.ShapeDtypeStruct(queries.shape, jnp.bfloat16),
        in_specs=[
            pl.BlockSpec(memory_space=pltpu.SMEM),
            pl.BlockSpec(memory_space=pl.ANY),
            pl.BlockSpec(memory_space=pl.ANY),
            pl.BlockSpec(memory_space=pl.ANY),
        ],
        out_specs=pl.BlockSpec(memory_space=pltpu.VMEM),
        scratch_shapes=[
            pltpu.VMEM((n, pieces, 2, group_blocks, block_len, HD), jnp.bfloat16),
            pltpu.VMEM((groups, per_group, rows, HD), jnp.bfloat16),
            pltpu.VMEM((groups, group_rows, 2 * HD), jnp.float32),
            pltpu.VMEM((groups, group_rows, HD), jnp.float32),
            pltpu.VMEM((per_group, rows, HD), jnp.bfloat16),
            pltpu.VMEM((2, per_group, HD), jnp.float32),
            pltpu.VMEM((per_group, rows, HD), jnp.bfloat16),
            pltpu.VMEM((2, per_group, HD), jnp.float32),
            pltpu.SemaphoreType.DMA((4 * pieces,)),
            pltpu.SemaphoreType.DMA((kv_heads * per_group,)),
            pltpu.SemaphoreType.DMA((2, n, pieces)),
            pltpu.SemaphoreType.DMA((n, pieces)),
            pltpu.SemaphoreType.DMA((3,)),
            pltpu.SemaphoreType.DMA((3,)),
        ],
        compiler_params=pltpu.CompilerParams(
            collective_id=0, has_side_effects=True, vmem_limit_bytes=60 * 1024 * 1024
        ),
        cost_estimate=pl.CostEstimate(
            flops=4 * work, bytes_accessed=4 * queries.size, transcendentals=work // HD
        ),
        name="context_attention",
    )(span_order, queries, new_kv, pool)


def solution(mesh):
    return jax.shard_map(
        local,
        mesh=mesh,
        in_specs=(
            P(("group", "ctx"), ("head", "pool")),
            P(None, ("group", "ctx"), ("head", "pool")),
            P(None, ("group", "ctx"), None, ("head", "pool")),
            P("group"),
            P("group"),
        ),
        out_specs=P(("group", "ctx"), ("head", "pool")),
        check_vma=False,
    )
```

```python
import functools
import math

import jax
import jax.numpy as jnp
from jax import lax
from jax.experimental import pallas as pl
from jax.experimental.pallas import tpu as pltpu
from jax.sharding import PartitionSpec as P

HD = 128
QH = 64
KVH = 8
CAP = 2


masked_score = -1e30


def lookup(indices, table):
    slots = jnp.arange(table.shape[0], dtype=jnp.int32)
    return jnp.sum(jnp.where(indices[:, None] == slots[None, :], table[None, :], 0), axis=1)


def key_positions(row_count, resident_rows, prefix_rows_dev, span_order, queries_dev, prefix_total):
    global_row = jnp.arange(row_count, dtype=jnp.int32)
    owner_index = global_row // resident_rows
    offset = global_row - owner_index * resident_rows
    span_index = lookup(owner_index, span_order)
    from_new = prefix_total + span_index * queries_dev + offset - prefix_rows_dev
    return jnp.where(offset < prefix_rows_dev, owner_index * prefix_rows_dev + offset, from_new)


def attend(state_now, query_rows, query_pos, kv_piece, key_pos, score_scale):
    acc_out, acc_max, acc_sum = state_now
    kv_heads = query_rows.shape[0]
    head_dim = query_rows.shape[2]
    row_count = kv_piece.shape[1]
    key_block = kv_piece[0].reshape(row_count, kv_heads, head_dim)
    value_block = kv_piece[1].reshape(row_count, kv_heads, head_dim)
    scores = (
        lax.dot_general(
            query_rows, key_block, (((2,), (2,)), ((0,), (1,))), preferred_element_type=jnp.float32
        )
        * score_scale
    )
    allowed = key_pos[None, None, :] <= query_pos[None, :, None]
    scores = jnp.where(allowed, scores, masked_score)
    new_max = jnp.maximum(acc_max, jnp.max(scores, axis=2))
    correct = jnp.exp(acc_max - new_max)
    exp_scores = jnp.where(allowed, jnp.exp(scores - new_max[:, :, None]), 0.0)
    new_sum = acc_sum * correct + jnp.sum(exp_scores, axis=2)
    weights = exp_scores.astype(jnp.bfloat16)
    update = lax.dot_general(
        weights, value_block, (((2,), (0,)), ((0,), (1,))), preferred_element_type=jnp.float32
    )
    return (acc_out * correct[:, :, None] + update, new_max, new_sum)


def attend_piece(state_now, query_rows, query_pos, kv_piece, key_pos, score_scale):
    row_count = kv_piece.shape[1]
    block_rows = row_count
    while block_rows > 2048 and block_rows % 2 == 0:
        block_rows = block_rows // 2
    block_count = row_count // block_rows
    blocks = jnp.moveaxis(kv_piece.reshape(2, block_count, block_rows, kv_piece.shape[2]), 1, 0)
    positions = key_pos.reshape(block_count, block_rows)

    def one_block(state_inner, block_item):
        return (
            attend(state_inner, query_rows, query_pos, block_item[0], block_item[1], score_scale),
            None,
        )

    final_state, unused = lax.scan(one_block, state_now, (blocks, positions))
    return final_state


def routed(queries, new_kv, pool, block_table, span_order):
    cycle_size = lax.axis_size("ctx")
    my_index = lax.axis_index("ctx")
    per_group = QH // KVH
    queries_dev = queries.shape[0]
    kv_heads = new_kv.shape[2] // HD
    pool_dev = pool.shape[1]
    block_len = pool.shape[2]
    blocks_dev = block_table.shape[0] // cycle_size
    owner_table = block_table.reshape(cycle_size, blocks_dev)
    holder = owner_table // pool_dev
    local_id = owner_table - holder * pool_dev
    same_holder = holder[:, :, None] == holder[:, None, :]
    earlier = (
        jnp.arange(blocks_dev, dtype=jnp.int32)[:, None]
        < jnp.arange(blocks_dev, dtype=jnp.int32)[None, :]
    )
    rank_in_list = jnp.sum((same_holder & earlier[None, :, :]).astype(jnp.int32), axis=1)
    slot_match = (holder[:, None, :] == my_index) & (
        rank_in_list[:, None, :] == jnp.arange(CAP, dtype=jnp.int32)[None, :, None]
    )
    source = jnp.sum(jnp.where(slot_match, local_id[:, None, :], 0), axis=2)
    filled = jnp.any(slot_match, axis=2)
    picked = jnp.take(pool, source.reshape(-1), axis=1)
    picked = jnp.where(filled.reshape(1, -1, 1, 1), picked, jnp.zeros_like(picked))
    outgoing = picked.reshape(2, cycle_size, CAP, block_len, pool.shape[3])
    incoming = lax.all_to_all(outgoing, "ctx", split_axis=1, concat_axis=1, tiled=True)
    my_holder = lax.dynamic_index_in_dim(holder, my_index, 0, keepdims=False)
    my_rank = lax.dynamic_index_in_dim(rank_in_list, my_index, 0, keepdims=False)
    flat_slot = my_holder * CAP + my_rank
    arrived = incoming.reshape(2, cycle_size * CAP, block_len, pool.shape[3])
    prefix_kv = jnp.take(arrived, flat_slot, axis=1).reshape(
        2, blocks_dev * block_len, pool.shape[3]
    )
    resident = jnp.concatenate([prefix_kv, new_kv], axis=1)
    resident_rows = resident.shape[1]
    prefix_rows_dev = blocks_dev * block_len
    prefix_total = cycle_size * prefix_rows_dev
    score_scale = 1.0 / math.sqrt(HD)
    row_offsets = jnp.arange(queries_dev, dtype=jnp.int32)
    own_span = lookup(my_index[None], span_order)[0]
    own_pos = jnp.repeat(prefix_total + own_span * queries_dev + row_offsets, per_group)
    query_rows = (
        queries.reshape(queries_dev, kv_heads, per_group, HD)
        .transpose(1, 0, 2, 3)
        .reshape(kv_heads, queries_dev * per_group, HD)
    )
    grouped_rows = queries_dev * per_group
    start_state = (
        jnp.zeros((kv_heads, grouped_rows, HD), jnp.float32),
        jnp.full((kv_heads, grouped_rows), masked_score, jnp.float32),
        jnp.zeros((kv_heads, grouped_rows), jnp.float32),
    )
    kv_piece = lax.all_gather(resident, "ctx", axis=1, tiled=True)
    positions = key_positions(
        kv_piece.shape[1], resident_rows, prefix_rows_dev, span_order, queries_dev, prefix_total
    )
    final_state = attend_piece(start_state, query_rows, own_pos, kv_piece, positions, score_scale)
    out_sum, out_max, out_total = final_state
    result = out_sum / out_total[:, :, None]
    result = (
        result.reshape(kv_heads, queries_dev, per_group, HD)
        .transpose(1, 0, 2, 3)
        .reshape(queries_dev, kv_heads * per_group * HD)
    )
    return result.astype(jnp.bfloat16)


def context_kernel(
    n, kv_heads, per_group, splits,
    span_ref, queries_ref, new_ref, pool_ref, out_ref,
    kv, qs, acc, row_max, part_out, part_stat, got_out, got_stat,
    load_sem, query_sem, kv_send, kv_recv, ask_send, ask_recv,
    part_send, part_recv, stat_send, stat_recv,
):
    me = lax.axis_index("ctx")
    at_edge = (me == 0) | (me == n - 1)
    inner = jnp.logical_not(at_edge)
    mate = jnp.where(me % 2 == 0, me + 1, me - 1)
    across = n - 1 - me
    far = n - 1 - mate
    helper = jnp.where(at_edge, far, across)
    my_role = jnp.where(at_edge, 2, 1)
    pool_dev, block_len = pool_ref.shape[1], pool_ref.shape[2]
    pieces, group_blocks = kv.shape[1], kv.shape[3]
    keys = group_blocks * block_len
    rows = queries_ref.shape[0]
    tile_heads = 2 if per_group % 2 == 0 else 1
    tile_rows = tile_heads * rows
    tiles = per_group // tile_heads
    unit = math.log2(math.e) / math.sqrt(HD)
    MESH = pl.DeviceIdType.MESH

    def asker_of(role):
        return jnp.where(role == 0, me, jnp.where(role == 1, across, far))

    loads = [[] for _ in range(pieces)]
    count = 0
    for piece in range(pieces):
        kv_head, split = divmod(piece, splits)
        columns = pl.ds(kv_head * HD, HD)
        first = split * group_blocks
        pool_blocks = min(group_blocks, pool_dev - first)
        for t in range(2):
            if pool_blocks > 0:
                loads[piece].append(
                    pltpu.make_async_copy(
                        pool_ref.at[t, pl.ds(first, pool_blocks), :, columns],
                        kv.at[0, piece, t, pl.ds(0, pool_blocks)],
                        load_sem.at[count],
                    )
                )
                count += 1
            if pool_blocks < group_blocks:
                loads[piece].append(
                    pltpu.make_async_copy(
                        new_ref.at[t, :, columns],
                        kv.at[0, piece, t, group_blocks - 1],
                        load_sem.at[count],
                    )
                )
                count += 1
    for piece in range(pieces):
        for load in loads[piece]:
            load.start()
    query_loads = []
    for head in range(kv_heads):
        for member in range(per_group):
            query_loads.append(
                pltpu.make_async_copy(
                    queries_ref.at[:, pl.ds((head * per_group + member) * HD, HD)],
                    qs.at[0, head, member],
                    query_sem.at[head * per_group + member],
                )
            )
            query_loads[-1].start()

    barrier = pltpu.get_barrier_semaphore()
    pl.semaphore_signal(barrier, inc=1, device_id={"ctx": mate}, device_id_type=MESH)
    pl.semaphore_signal(barrier, inc=1, device_id={"ctx": helper}, device_id_type=MESH)

    @pl.when(inner)
    def _():
        pl.semaphore_signal(barrier, inc=1, device_id={"ctx": far}, device_id_type=MESH)
        pl.semaphore_wait(barrier, 3)

    @pl.when(at_edge)
    def _():
        pl.semaphore_wait(barrier, 2)

    def kv_copy(piece):
        return pltpu.make_async_remote_copy(
            src_ref=kv.at[0, piece],
            dst_ref=kv.at[1, piece],
            send_sem=kv_send.at[piece],
            recv_sem=kv_recv.at[piece],
            device_id={"ctx": mate},
            device_id_type=MESH,
        )

    def ask_copy(head, role):
        return pltpu.make_async_remote_copy(
            src_ref=qs.at[0, head],
            dst_ref=qs.at[role, head],
            send_sem=ask_send.at[head],
            recv_sem=ask_recv.at[role - 1, head],
            device_id={"ctx": helper},
            device_id_type=MESH,
        )

    def part_copies(role, head):
        target = jnp.where(role == 1, across, far)
        return (
            pltpu.make_async_remote_copy(
                src_ref=part_out.at[role - 1, head],
                dst_ref=got_out.at[head],
                send_sem=part_send.at[role - 1, head],
                recv_sem=part_recv.at[head],
                device_id={"ctx": target},
                device_id_type=MESH,
            ),
            pltpu.make_async_remote_copy(
                src_ref=part_stat.at[role - 1, head],
                dst_ref=got_stat.at[head],
                send_sem=stat_send.at[role - 1, head],
                recv_sem=stat_recv.at[head],
                device_id={"ctx": target},
                device_id_type=MESH,
            ),
        )

    last_head = kv_heads - 1
    held_back = last_head * splits

    def ask_all():
        for head in range(kv_heads):
            for load in query_loads[head * per_group : (head + 1) * per_group]:
                load.wait()
            ask_copy(head, my_role).start()

    @pl.when(inner)
    def _():
        ask_all()

    for piece in range(pieces):
        for load in loads[piece]:
            load.wait()
        if piece < held_back:
            kv_copy(piece).start()

    @pl.when(at_edge)
    def _():
        ask_all()

    @pl.when(inner)
    def _():
        for piece in range(held_back, pieces):
            kv_copy(piece).start()

    query_row = lax.broadcasted_iota(jnp.int32, (tile_heads, rows, block_len), 1).reshape(
        tile_rows, block_len
    )
    key_column = lax.broadcasted_iota(jnp.int32, (tile_rows, block_len), 1)
    offset = key_column - query_row

    def attend_tiles(role, head, slot, split, count, fresh=False):
        taken = pl.ds(head * splits + split, count)
        width = count * keys
        key_rows = kv[slot, taken, 0].reshape(width, HD)
        value_rows = kv[slot, taken, 1].reshape(width, HD)
        value_ones = jnp.concatenate([value_rows, jnp.ones_like(value_rows)], axis=1)
        limit = (span_ref[asker_of(role)] - span_ref[jnp.where(slot == 0, me, mate)]) * rows
        if count < splits:
            has_new = split == splits - 1
            limit = jnp.where(has_new, limit, rows + block_len)
        allowed = offset <= limit
        for tile in range(tiles):
            heads = pl.ds(tile * tile_heads, tile_heads)
            query_tile = qs[role, head, heads].reshape(tile_rows, HD)
            scores = lax.dot_general(
                query_tile, key_rows, (((1,), (1,)), ((), ())), preferred_element_type=jnp.float32
            )
            last = jnp.where(allowed, scores[:, width - block_len :], masked_score)
            scores = jnp.concatenate([scores[:, : width - block_len], last], axis=1)
            span = pl.ds(tile * tile_rows, tile_rows)
            new_max = jnp.max(scores, axis=1, keepdims=True)
            if fresh:
                new_max = jnp.broadcast_to(new_max, (tile_rows, HD))
            else:
                old_max = row_max[role, head, span]
                new_max = jnp.maximum(old_max, new_max)
            row_max[role, head, span] = new_max
            wide = jnp.concatenate([new_max] * (width // HD), axis=1)
            weights = jnp.exp2((scores - wide) * unit).astype(jnp.bfloat16)
            update = jnp.dot(weights, value_ones, preferred_element_type=jnp.float32)
            if not fresh:
                correct = jnp.exp2((old_max - new_max) * unit)
                update += acc[role, head, span] * jnp.concatenate([correct, correct], axis=1)
            acc[role, head, span] = update

    diagonal = lax.broadcasted_iota(jnp.int32, (rows, HD), 0) == lax.broadcasted_iota(
        jnp.int32, (rows, HD), 1
    )

    def return_part(role, head):
        for member in range(per_group):
            span = pl.ds(member * rows, rows)
            total = acc[role, head, span, HD:]
            part_out[role - 1, head, member] = (acc[role, head, span, :HD] / total).astype(
                jnp.bfloat16
            )
            peak = row_max[role, head, span]
            part_stat[role - 1, head, 0, pl.ds(member, 1)] = jnp.sum(
                jnp.where(diagonal, peak, 0.0), axis=0, keepdims=True
            )
            part_stat[role - 1, head, 1, pl.ds(member, 1)] = jnp.sum(
                jnp.where(diagonal, total, 0.0), axis=0, keepdims=True
            )
        for copy in part_copies(role, head):
            copy.start()

    def near_keys(step, carry):
        role, head = step // kv_heads, step % kv_heads

        @pl.when((role == 0) | inner)
        def _():
            @pl.when(role == 1)
            def _():
                ask_copy(head, 1).wait_recv()

            attend_tiles(role, head, 0, 0, splits, fresh=True)

        return carry

    lax.fori_loop(0, 2 * kv_heads, near_keys, 0)

    @pl.when(at_edge)
    def _():
        for piece in range(held_back):
            kv_copy(piece).wait_send()
        for piece in range(held_back, pieces):
            kv_copy(piece).start()

    for head in range(last_head):
        for split in range(splits):
            kv_copy(head * splits + split).wait_recv()

        def one_role(step, carry, head=head):
            role = (step + 1) % 3

            @pl.when((role == 0) | inner)
            def _():
                @pl.when(role == 2)
                def _():
                    ask_copy(head, 2).wait_recv()
                    attend_tiles(role, head, 0, 0, splits, fresh=True)

                attend_tiles(role, head, 1, 0, splits)

                @pl.when(role > 0)
                def _():
                    return_part(role, head)

            return carry

        lax.fori_loop(0, 3, one_role, 0)

    @pl.when(inner)
    def _():
        ask_copy(last_head, 2).wait_recv()
        attend_tiles(2, last_head, 0, 0, splits, fresh=True)

    def last_pieces(step, carry):
        split, role = step // 3, (step + 1) % 3

        @pl.when(role == 1)
        def _():
            kv_copy(held_back + split).wait_recv()

        @pl.when((role == 0) | inner)
        def _():
            attend_tiles(role, last_head, 1, split, 1)

            @pl.when((role > 0) & (split == splits - 1))
            def _():
                return_part(role, last_head)

        return carry

    lax.fori_loop(0, 3 * splits, last_pieces, 0)

    def settle(head, member):
        span = pl.ds(member * rows, rows)
        their_max = jnp.broadcast_to(got_stat[head, 0, pl.ds(member, 1)], (HD, rows)).T
        their_total = jnp.broadcast_to(got_stat[head, 1, pl.ds(member, 1)], (HD, rows)).T
        my_max = row_max[0, head, span]
        top = jnp.maximum(my_max, their_max)
        mine = jnp.exp2((my_max - top) * unit)
        theirs = jnp.exp2((their_max - top) * unit) * their_total
        total = acc[0, head, span, HD:] * mine + theirs
        summed = acc[0, head, span, :HD] * mine + got_out[head, member].astype(jnp.float32) * theirs
        columns = pl.ds((head * per_group + member) * HD, HD)
        out_ref[:, columns] = (summed / total).astype(out_ref.dtype)

    for head in range(kv_heads):
        for copy in part_copies(my_role, head):
            copy.wait_recv()
        for member in range(per_group):
            settle(head, member)

    @pl.when(inner)
    def _():
        for piece in range(held_back):
            kv_copy(piece).wait_send()
        for role in (1, 2):
            for head in range(kv_heads):
                for copy in part_copies(role, head):
                    copy.wait_send()

    for piece in range(held_back, pieces):
        kv_copy(piece).wait_send()
    for head in range(kv_heads):
        ask_copy(head, my_role).wait_send()


def local(queries, new_kv, pool, block_table, span_order):
    n = lax.axis_size("ctx")
    pool_dev, block_len = pool.shape[1], pool.shape[2]
    rows = queries.shape[0]
    kv_heads = new_kv.shape[2] // HD
    per_group = QH // KVH
    whole_pool = block_table.shape[0] == n * pool_dev
    if not whole_pool or n != 4 or rows != block_len or rows != HD:
        return routed(queries, new_kv, pool, block_table, span_order)
    blocks = pool_dev + 1
    splits = 3 if blocks % 3 == 0 and blocks > 3 else 1
    pieces = kv_heads * splits
    group_blocks = blocks // splits
    group_rows = per_group * rows
    work = queries.shape[1] * rows * block_len * blocks * n
    return pl.pallas_call(
        functools.partial(context_kernel, n, kv_heads, per_group, splits),
        out_shape=jax.ShapeDtypeStruct(queries.shape, jnp.bfloat16),
        in_specs=[
            pl.BlockSpec(memory_space=pltpu.SMEM),
            pl.BlockSpec(memory_space=pl.ANY),
            pl.BlockSpec(memory_space=pl.ANY),
            pl.BlockSpec(memory_space=pl.ANY),
        ],
        out_specs=pl.BlockSpec(memory_space=pltpu.VMEM),
        scratch_shapes=[
            pltpu.VMEM((2, pieces, 2, group_blocks, block_len, HD), jnp.bfloat16),
            pltpu.VMEM((3, kv_heads, per_group, rows, HD), jnp.bfloat16),
            pltpu.VMEM((3, kv_heads, group_rows, 2 * HD), jnp.float32),
            pltpu.VMEM((3, kv_heads, group_rows, HD), jnp.float32),
            pltpu.VMEM((2, kv_heads, per_group, rows, HD), jnp.bfloat16),
            pltpu.VMEM((2, kv_heads, 2, per_group, HD), jnp.float32),
            pltpu.VMEM((kv_heads, per_group, rows, HD), jnp.bfloat16),
            pltpu.VMEM((kv_heads, 2, per_group, HD), jnp.float32),
            pltpu.SemaphoreType.DMA((4 * pieces,)),
            pltpu.SemaphoreType.DMA((kv_heads * per_group,)),
            pltpu.SemaphoreType.DMA((pieces,)),
            pltpu.SemaphoreType.DMA((pieces,)),
            pltpu.SemaphoreType.DMA((kv_heads,)),
            pltpu.SemaphoreType.DMA((2, kv_heads)),
            pltpu.SemaphoreType.DMA((2, kv_heads)),
            pltpu.SemaphoreType.DMA((kv_heads,)),
            pltpu.SemaphoreType.DMA((2, kv_heads)),
            pltpu.SemaphoreType.DMA((kv_heads,)),
        ],
        compiler_params=pltpu.CompilerParams(
            collective_id=0, has_side_effects=True, vmem_limit_bytes=60 * 1024 * 1024
        ),
        cost_estimate=pl.CostEstimate(
            flops=4 * work, bytes_accessed=4 * queries.size, transcendentals=work // HD
        ),
        name="context_attention",
    )(span_order, queries, new_kv, pool)


def solution(mesh):
    return jax.shard_map(
        local,
        mesh=mesh,
        in_specs=(
            P(("group", "ctx"), ("head", "pool")),
            P(None, ("group", "ctx"), ("head", "pool")),
            P(None, ("group", "ctx"), None, ("head", "pool")),
            P("group"),
            P("group"),
        ),
        out_specs=P(("group", "ctx"), ("head", "pool")),
        check_vma=False,
    )
```

```python
import functools
import math

import jax
import jax.numpy as jnp
from jax import lax
from jax.experimental import pallas as pl
from jax.experimental.pallas import tpu as pltpu
from jax.sharding import PartitionSpec as P

HD = 128
QH = 64
KVH = 8
CAP = 2


masked_score = -1e30


def lookup(indices, table):
    slots = jnp.arange(table.shape[0], dtype=jnp.int32)
    return jnp.sum(jnp.where(indices[:, None] == slots[None, :], table[None, :], 0), axis=1)


def key_positions(row_count, resident_rows, prefix_rows_dev, span_order, queries_dev, prefix_total):
    global_row = jnp.arange(row_count, dtype=jnp.int32)
    owner_index = global_row // resident_rows
    offset = global_row - owner_index * resident_rows
    span_index = lookup(owner_index, span_order)
    from_new = prefix_total + span_index * queries_dev + offset - prefix_rows_dev
    return jnp.where(offset < prefix_rows_dev, owner_index * prefix_rows_dev + offset, from_new)


def attend(state_now, query_rows, query_pos, kv_piece, key_pos, score_scale):
    acc_out, acc_max, acc_sum = state_now
    kv_heads = query_rows.shape[0]
    head_dim = query_rows.shape[2]
    row_count = kv_piece.shape[1]
    key_block = kv_piece[0].reshape(row_count, kv_heads, head_dim)
    value_block = kv_piece[1].reshape(row_count, kv_heads, head_dim)
    scores = (
        lax.dot_general(
            query_rows, key_block, (((2,), (2,)), ((0,), (1,))), preferred_element_type=jnp.float32
        )
        * score_scale
    )
    allowed = key_pos[None, None, :] <= query_pos[None, :, None]
    scores = jnp.where(allowed, scores, masked_score)
    new_max = jnp.maximum(acc_max, jnp.max(scores, axis=2))
    correct = jnp.exp(acc_max - new_max)
    exp_scores = jnp.where(allowed, jnp.exp(scores - new_max[:, :, None]), 0.0)
    new_sum = acc_sum * correct + jnp.sum(exp_scores, axis=2)
    weights = exp_scores.astype(jnp.bfloat16)
    update = lax.dot_general(
        weights, value_block, (((2,), (0,)), ((0,), (1,))), preferred_element_type=jnp.float32
    )
    return (acc_out * correct[:, :, None] + update, new_max, new_sum)


def attend_piece(state_now, query_rows, query_pos, kv_piece, key_pos, score_scale):
    row_count = kv_piece.shape[1]
    block_rows = row_count
    while block_rows > 2048 and block_rows % 2 == 0:
        block_rows = block_rows // 2
    block_count = row_count // block_rows
    blocks = jnp.moveaxis(kv_piece.reshape(2, block_count, block_rows, kv_piece.shape[2]), 1, 0)
    positions = key_pos.reshape(block_count, block_rows)

    def one_block(state_inner, block_item):
        return (
            attend(state_inner, query_rows, query_pos, block_item[0], block_item[1], score_scale),
            None,
        )

    final_state, unused = lax.scan(one_block, state_now, (blocks, positions))
    return final_state


def routed(queries, new_kv, pool, block_table, span_order):
    cycle_size = lax.axis_size("ctx")
    my_index = lax.axis_index("ctx")
    per_group = QH // KVH
    queries_dev = queries.shape[0]
    kv_heads = new_kv.shape[2] // HD
    pool_dev = pool.shape[1]
    block_len = pool.shape[2]
    blocks_dev = block_table.shape[0] // cycle_size
    owner_table = block_table.reshape(cycle_size, blocks_dev)
    holder = owner_table // pool_dev
    local_id = owner_table - holder * pool_dev
    same_holder = holder[:, :, None] == holder[:, None, :]
    earlier = (
        jnp.arange(blocks_dev, dtype=jnp.int32)[:, None]
        < jnp.arange(blocks_dev, dtype=jnp.int32)[None, :]
    )
    rank_in_list = jnp.sum((same_holder & earlier[None, :, :]).astype(jnp.int32), axis=1)
    slot_match = (holder[:, None, :] == my_index) & (
        rank_in_list[:, None, :] == jnp.arange(CAP, dtype=jnp.int32)[None, :, None]
    )
    source = jnp.sum(jnp.where(slot_match, local_id[:, None, :], 0), axis=2)
    filled = jnp.any(slot_match, axis=2)
    picked = jnp.take(pool, source.reshape(-1), axis=1)
    picked = jnp.where(filled.reshape(1, -1, 1, 1), picked, jnp.zeros_like(picked))
    outgoing = picked.reshape(2, cycle_size, CAP, block_len, pool.shape[3])
    incoming = lax.all_to_all(outgoing, "ctx", split_axis=1, concat_axis=1, tiled=True)
    my_holder = lax.dynamic_index_in_dim(holder, my_index, 0, keepdims=False)
    my_rank = lax.dynamic_index_in_dim(rank_in_list, my_index, 0, keepdims=False)
    flat_slot = my_holder * CAP + my_rank
    arrived = incoming.reshape(2, cycle_size * CAP, block_len, pool.shape[3])
    prefix_kv = jnp.take(arrived, flat_slot, axis=1).reshape(
        2, blocks_dev * block_len, pool.shape[3]
    )
    resident = jnp.concatenate([prefix_kv, new_kv], axis=1)
    resident_rows = resident.shape[1]
    prefix_rows_dev = blocks_dev * block_len
    prefix_total = cycle_size * prefix_rows_dev
    score_scale = 1.0 / math.sqrt(HD)
    row_offsets = jnp.arange(queries_dev, dtype=jnp.int32)
    own_span = lookup(my_index[None], span_order)[0]
    own_pos = jnp.repeat(prefix_total + own_span * queries_dev + row_offsets, per_group)
    query_rows = (
        queries.reshape(queries_dev, kv_heads, per_group, HD)
        .transpose(1, 0, 2, 3)
        .reshape(kv_heads, queries_dev * per_group, HD)
    )
    grouped_rows = queries_dev * per_group
    start_state = (
        jnp.zeros((kv_heads, grouped_rows, HD), jnp.float32),
        jnp.full((kv_heads, grouped_rows), masked_score, jnp.float32),
        jnp.zeros((kv_heads, grouped_rows), jnp.float32),
    )
    kv_piece = lax.all_gather(resident, "ctx", axis=1, tiled=True)
    positions = key_positions(
        kv_piece.shape[1], resident_rows, prefix_rows_dev, span_order, queries_dev, prefix_total
    )
    final_state = attend_piece(start_state, query_rows, own_pos, kv_piece, positions, score_scale)
    out_sum, out_max, out_total = final_state
    result = out_sum / out_total[:, :, None]
    result = (
        result.reshape(kv_heads, queries_dev, per_group, HD)
        .transpose(1, 0, 2, 3)
        .reshape(queries_dev, kv_heads * per_group * HD)
    )
    return result.astype(jnp.bfloat16)


def context_kernel(
    n, kv_heads, per_group, splits,
    order_ref, queries_ref, new_ref, pool_ref, out_ref,
    span_ref,
    kv, qs, acc, row_max, part_out, part_stat, got_out, got_stat,
    order_sem, load_sem, query_sem, kv_send, kv_recv, ask_send, ask_recv,
    part_send, part_recv, stat_send, stat_recv,
):
    me = lax.axis_index("ctx")
    at_edge = (me == 0) | (me == n - 1)
    inner = jnp.logical_not(at_edge)
    mate = jnp.where(me % 2 == 0, me + 1, me - 1)
    across = n - 1 - me
    far = n - 1 - mate
    helper = jnp.where(at_edge, far, across)
    my_role = jnp.where(at_edge, 2, 1)
    pool_dev, block_len = pool_ref.shape[1], pool_ref.shape[2]
    pieces, group_blocks = kv.shape[1], kv.shape[3]
    keys = group_blocks * block_len
    rows = queries_ref.shape[0]
    tile_heads = 2 if per_group % 2 == 0 else 1
    tile_rows = tile_heads * rows
    tiles = per_group // tile_heads
    halves = part_out.shape[2]
    half_heads = per_group // halves
    unit = math.log2(math.e) / math.sqrt(HD)
    MESH = pl.DeviceIdType.MESH

    def asker_of(role):
        return jnp.where(role == 0, me, jnp.where(role == 1, across, far))

    loads = [[] for _ in range(pieces)]
    count = 0
    for piece in range(pieces):
        kv_head, split = divmod(piece, splits)
        columns = pl.ds(kv_head * HD, HD)
        first = split * group_blocks
        pool_blocks = min(group_blocks, pool_dev - first)
        for t in range(2):
            if pool_blocks > 0:
                loads[piece].append(
                    pltpu.make_async_copy(
                        pool_ref.at[t, pl.ds(first, pool_blocks), :, columns],
                        kv.at[0, piece, t, pl.ds(0, pool_blocks)],
                        load_sem.at[count],
                    )
                )
                count += 1
            if pool_blocks < group_blocks:
                loads[piece].append(
                    pltpu.make_async_copy(
                        new_ref.at[t, :, columns],
                        kv.at[0, piece, t, group_blocks - 1],
                        load_sem.at[count],
                    )
                )
                count += 1
    for piece in range(pieces):
        for load in loads[piece]:
            load.start()
    order_load = pltpu.make_async_copy(order_ref, span_ref, order_sem)
    order_load.start()
    query_loads = []
    for head in range(kv_heads):
        for member in range(per_group):
            query_loads.append(
                pltpu.make_async_copy(
                    queries_ref.at[:, pl.ds((head * per_group + member) * HD, HD)],
                    qs.at[0, head, member],
                    query_sem.at[head * per_group + member],
                )
            )
            query_loads[-1].start()

    barrier = pltpu.get_barrier_semaphore()
    pl.semaphore_signal(barrier, inc=1, device_id={"ctx": mate}, device_id_type=MESH)
    pl.semaphore_signal(barrier, inc=1, device_id={"ctx": helper}, device_id_type=MESH)

    @pl.when(inner)
    def _():
        pl.semaphore_signal(barrier, inc=1, device_id={"ctx": far}, device_id_type=MESH)
        pl.semaphore_wait(barrier, 3)

    @pl.when(at_edge)
    def _():
        pl.semaphore_wait(barrier, 2)

    def kv_copy(piece):
        return pltpu.make_async_remote_copy(
            src_ref=kv.at[0, piece],
            dst_ref=kv.at[1, piece],
            send_sem=kv_send.at[piece],
            recv_sem=kv_recv.at[piece],
            device_id={"ctx": mate},
            device_id_type=MESH,
        )

    def ask_copy(head, role):
        return pltpu.make_async_remote_copy(
            src_ref=qs.at[0, head],
            dst_ref=qs.at[role, head],
            send_sem=ask_send.at[head],
            recv_sem=ask_recv.at[role - 1, head],
            device_id={"ctx": helper},
            device_id_type=MESH,
        )

    def part_copies(role, head, half):
        target = jnp.where(role == 1, across, far)
        return (
            pltpu.make_async_remote_copy(
                src_ref=part_out.at[role - 1, head, half],
                dst_ref=got_out.at[head, half],
                send_sem=part_send.at[role - 1, head, half],
                recv_sem=part_recv.at[head, half],
                device_id={"ctx": target},
                device_id_type=MESH,
            ),
            pltpu.make_async_remote_copy(
                src_ref=part_stat.at[role - 1, head, half],
                dst_ref=got_stat.at[head, half],
                send_sem=stat_send.at[role - 1, head, half],
                recv_sem=stat_recv.at[head, half],
                device_id={"ctx": target},
                device_id_type=MESH,
            ),
        )

    last_head = kv_heads - 1
    held_back = last_head * splits

    def ask_all():
        for head in range(kv_heads):
            for load in query_loads[head * per_group : (head + 1) * per_group]:
                load.wait()
            ask_copy(head, my_role).start()

    @pl.when(inner)
    def _():
        ask_all()

    for piece in range(pieces):
        for load in loads[piece]:
            load.wait()
        if piece < held_back:
            kv_copy(piece).start()

    @pl.when(at_edge)
    def _():
        ask_all()

    @pl.when(inner)
    def _():
        for piece in range(held_back, pieces):
            kv_copy(piece).start()

    query_row = lax.broadcasted_iota(jnp.int32, (tile_heads, rows, block_len), 1).reshape(
        tile_rows, block_len
    )
    key_column = lax.broadcasted_iota(jnp.int32, (tile_rows, block_len), 1)
    offset = key_column - query_row

    def attend_tiles(role, head, slot, split, count, fresh=False, half=None):
        taken = pl.ds(head * splits + split, count)
        width = count * keys
        key_rows = kv[slot, taken, 0].reshape(width, HD)
        value_rows = kv[slot, taken, 1].reshape(width, HD)
        value_ones = jnp.concatenate([value_rows, jnp.ones_like(value_rows)], axis=1)
        limit = (span_ref[asker_of(role)] - span_ref[jnp.where(slot == 0, me, mate)]) * rows
        if count < splits:
            has_new = split == splits - 1
            limit = jnp.where(has_new, limit, rows + block_len)
        allowed = offset <= limit
        first_row = 0 if half is None else pl.multiple_of(half * (half_heads * rows), tile_rows)
        first_head = 0 if half is None else half * half_heads
        for tile in range(tiles if half is None else tiles // halves):
            heads = pl.ds(first_head + tile * tile_heads, tile_heads)
            query_tile = qs[role, head, heads].reshape(tile_rows, HD)
            scores = lax.dot_general(
                query_tile, key_rows, (((1,), (1,)), ((), ())), preferred_element_type=jnp.float32
            )
            last = jnp.where(allowed, scores[:, width - block_len :], masked_score)
            scores = jnp.concatenate([scores[:, : width - block_len], last], axis=1)
            span = pl.ds(first_row + tile * tile_rows, tile_rows)
            new_max = jnp.max(scores, axis=1, keepdims=True)
            if fresh:
                new_max = jnp.broadcast_to(new_max, (tile_rows, HD))
            else:
                old_max = row_max[role, head, span]
                new_max = jnp.maximum(old_max, new_max)
            row_max[role, head, span] = new_max
            wide = jnp.concatenate([new_max] * (width // HD), axis=1)
            weights = jnp.exp2((scores - wide) * unit).astype(jnp.bfloat16)
            update = jnp.dot(weights, value_ones, preferred_element_type=jnp.float32)
            if not fresh:
                correct = jnp.exp2((old_max - new_max) * unit)
                update += acc[role, head, span] * jnp.concatenate([correct, correct], axis=1)
            acc[role, head, span] = update

    diagonal = lax.broadcasted_iota(jnp.int32, (rows, HD), 0) == lax.broadcasted_iota(
        jnp.int32, (rows, HD), 1
    )

    def return_part(role, head, half):
        for member in range(half_heads):
            first = (half * half_heads + member) * rows
            span = pl.ds(pl.multiple_of(first, rows), rows)
            total = acc[role, head, span, HD:]
            part_out[role - 1, head, half, member] = (acc[role, head, span, :HD] / total).astype(
                jnp.bfloat16
            )
            peak = row_max[role, head, span]
            part_stat[role - 1, head, half, pl.ds(member, 1)] = jnp.sum(
                jnp.where(diagonal, peak, 0.0), axis=0, keepdims=True
            )
            part_stat[role - 1, head, half, pl.ds(half_heads + member, 1)] = jnp.sum(
                jnp.where(diagonal, total, 0.0), axis=0, keepdims=True
            )
        for copy in part_copies(role, head, half):
            copy.start()

    order_load.wait()

    def near_keys(step, carry):
        role, head = step // kv_heads, step % kv_heads

        @pl.when((role == 0) | inner)
        def _():
            @pl.when(role == 1)
            def _():
                ask_copy(head, 1).wait_recv()

            attend_tiles(role, head, 0, 0, splits, fresh=True)

        return carry

    lax.fori_loop(0, 2 * kv_heads, near_keys, 0)

    @pl.when(at_edge)
    def _():
        for piece in range(held_back):
            kv_copy(piece).wait_send()
        for piece in range(held_back, pieces):
            kv_copy(piece).start()

    for head in range(last_head):
        for split in range(splits):
            kv_copy(head * splits + split).wait_recv()

        def one_role(step, carry, head=head):
            role = (step + 1) % 3

            @pl.when((role == 0) | inner)
            def _():
                @pl.when(role == 2)
                def _():
                    ask_copy(head, 2).wait_recv()
                    attend_tiles(role, head, 0, 0, splits, fresh=True)

                attend_tiles(role, head, 1, 0, splits)

                @pl.when(role > 0)
                def _():
                    def one_half(half, carry):
                        return_part(role, head, half)
                        return carry

                    lax.fori_loop(0, halves, one_half, 0)

            return carry

        lax.fori_loop(0, 3, one_role, 0)

    @pl.when(inner)
    def _():
        ask_copy(last_head, 2).wait_recv()
        attend_tiles(2, last_head, 0, 0, splits, fresh=True)

    def last_pieces(step, carry):
        split, role = step // 3, (step + 1) % 3

        @pl.when(role == 1)
        def _():
            kv_copy(held_back + split).wait_recv()

        @pl.when((role == 0) | inner)
        def _():
            def one_half(half, carry):
                attend_tiles(role, last_head, 1, split, 1, half=half)

                @pl.when((role > 0) & (split == splits - 1))
                def _():
                    return_part(role, last_head, half)

                return carry

            lax.fori_loop(0, halves, one_half, 0)

        return carry

    lax.fori_loop(0, 3 * splits, last_pieces, 0)

    def settle(head, half, member):
        index = half * half_heads + member
        span = pl.ds(index * rows, rows)
        their_max = jnp.broadcast_to(got_stat[head, half, pl.ds(member, 1)], (HD, rows)).T
        their_total = jnp.broadcast_to(
            got_stat[head, half, pl.ds(half_heads + member, 1)], (HD, rows)
        ).T
        my_max = row_max[0, head, span]
        top = jnp.maximum(my_max, their_max)
        mine = jnp.exp2((my_max - top) * unit)
        theirs = jnp.exp2((their_max - top) * unit) * their_total
        total = acc[0, head, span, HD:] * mine + theirs
        summed = acc[0, head, span, :HD] * mine + got_out[head, half, member].astype(jnp.float32) * theirs
        columns = pl.ds((head * per_group + index) * HD, HD)
        out_ref[:, columns] = (summed / total).astype(out_ref.dtype)

    for head in range(kv_heads):
        for half in range(halves):
            for copy in part_copies(my_role, head, half):
                copy.wait_recv()
            for member in range(half_heads):
                settle(head, half, member)

    @pl.when(inner)
    def _():
        for piece in range(held_back):
            kv_copy(piece).wait_send()
        for role in (1, 2):
            for head in range(kv_heads):
                for half in range(halves):
                    for copy in part_copies(role, head, half):
                        copy.wait_send()

    for piece in range(held_back, pieces):
        kv_copy(piece).wait_send()
    for head in range(kv_heads):
        ask_copy(head, my_role).wait_send()


def local(queries, new_kv, pool, block_table, span_order):
    n = lax.axis_size("ctx")
    pool_dev, block_len = pool.shape[1], pool.shape[2]
    rows = queries.shape[0]
    kv_heads = new_kv.shape[2] // HD
    per_group = QH // KVH
    whole_pool = block_table.shape[0] == n * pool_dev
    if not whole_pool or n != 4 or rows != block_len or rows != HD:
        return routed(queries, new_kv, pool, block_table, span_order)
    blocks = pool_dev + 1
    splits = 3 if blocks % 3 == 0 and blocks > 3 else 1
    pieces = kv_heads * splits
    group_blocks = blocks // splits
    group_rows = per_group * rows
    halves = 2 if per_group % 4 == 0 else 1
    work = queries.shape[1] * rows * block_len * blocks * n
    return pl.pallas_call(
        functools.partial(context_kernel, n, kv_heads, per_group, splits),
        out_shape=jax.ShapeDtypeStruct(queries.shape, jnp.bfloat16),
        in_specs=[
            pl.BlockSpec(memory_space=pltpu.HBM),
            pl.BlockSpec(memory_space=pltpu.HBM),
            pl.BlockSpec(memory_space=pltpu.HBM),
            pl.BlockSpec(memory_space=pltpu.HBM),
        ],
        out_specs=pl.BlockSpec(memory_space=pltpu.VMEM),
        scratch_shapes=[
            pltpu.SMEM(span_order.shape, jnp.int32),
            pltpu.VMEM((2, pieces, 2, group_blocks, block_len, HD), jnp.bfloat16),
            pltpu.VMEM((3, kv_heads, per_group, rows, HD), jnp.bfloat16),
            pltpu.VMEM((3, kv_heads, group_rows, 2 * HD), jnp.float32),
            pltpu.VMEM((3, kv_heads, group_rows, HD), jnp.float32),
            pltpu.VMEM((2, kv_heads, halves, per_group // halves, rows, HD), jnp.bfloat16),
            pltpu.VMEM((2, kv_heads, halves, 2 * (per_group // halves), HD), jnp.float32),
            pltpu.VMEM((kv_heads, halves, per_group // halves, rows, HD), jnp.bfloat16),
            pltpu.VMEM((kv_heads, halves, 2 * (per_group // halves), HD), jnp.float32),
            pltpu.SemaphoreType.DMA,
            pltpu.SemaphoreType.DMA((4 * pieces,)),
            pltpu.SemaphoreType.DMA((kv_heads * per_group,)),
            pltpu.SemaphoreType.DMA((pieces,)),
            pltpu.SemaphoreType.DMA((pieces,)),
            pltpu.SemaphoreType.DMA((kv_heads,)),
            pltpu.SemaphoreType.DMA((2, kv_heads)),
            pltpu.SemaphoreType.DMA((2, kv_heads, halves)),
            pltpu.SemaphoreType.DMA((kv_heads, halves)),
            pltpu.SemaphoreType.DMA((2, kv_heads, halves)),
            pltpu.SemaphoreType.DMA((kv_heads, halves)),
        ],
        compiler_params=pltpu.CompilerParams(
            collective_id=0, has_side_effects=True, vmem_limit_bytes=40 * 1024 * 1024
        ),
        cost_estimate=pl.CostEstimate(
            flops=4 * work, bytes_accessed=4 * queries.size, transcendentals=work // HD
        ),
        name="context_attention",
    )(
        *(
            pltpu.with_memory_space_constraint(held, pltpu.HBM)
            for held in (span_order, queries, new_kv, pool)
        )
    )


def solution(mesh):
    return jax.shard_map(
        local,
        mesh=mesh,
        in_specs=(
            P(("group", "ctx"), ("head", "pool")),
            P(None, ("group", "ctx"), ("head", "pool")),
            P(None, ("group", "ctx"), None, ("head", "pool")),
            P("group"),
            P("group"),
        ),
        out_specs=P(("group", "ctx"), ("head", "pool")),
        check_vma=False,
    )
```

```python
import functools
import math

import jax
import jax.numpy as jnp
from jax import lax
from jax.experimental import pallas as pl
from jax.experimental.pallas import tpu as pltpu
from jax.sharding import PartitionSpec as P

HD = 128
QH = 64
KVH = 8
CAP = 2


masked_score = -1e30


def lookup(indices, table):
    slots = jnp.arange(table.shape[0], dtype=jnp.int32)
    return jnp.sum(jnp.where(indices[:, None] == slots[None, :], table[None, :], 0), axis=1)


def key_positions(row_count, resident_rows, prefix_rows_dev, span_order, queries_dev, prefix_total):
    global_row = jnp.arange(row_count, dtype=jnp.int32)
    owner_index = global_row // resident_rows
    offset = global_row - owner_index * resident_rows
    span_index = lookup(owner_index, span_order)
    from_new = prefix_total + span_index * queries_dev + offset - prefix_rows_dev
    return jnp.where(offset < prefix_rows_dev, owner_index * prefix_rows_dev + offset, from_new)


def attend(state_now, query_rows, query_pos, kv_piece, key_pos, score_scale):
    acc_out, acc_max, acc_sum = state_now
    kv_heads = query_rows.shape[0]
    head_dim = query_rows.shape[2]
    row_count = kv_piece.shape[1]
    key_block = kv_piece[0].reshape(row_count, kv_heads, head_dim)
    value_block = kv_piece[1].reshape(row_count, kv_heads, head_dim)
    scores = (
        lax.dot_general(
            query_rows, key_block, (((2,), (2,)), ((0,), (1,))), preferred_element_type=jnp.float32
        )
        * score_scale
    )
    allowed = key_pos[None, None, :] <= query_pos[None, :, None]
    scores = jnp.where(allowed, scores, masked_score)
    new_max = jnp.maximum(acc_max, jnp.max(scores, axis=2))
    correct = jnp.exp(acc_max - new_max)
    exp_scores = jnp.where(allowed, jnp.exp(scores - new_max[:, :, None]), 0.0)
    new_sum = acc_sum * correct + jnp.sum(exp_scores, axis=2)
    weights = exp_scores.astype(jnp.bfloat16)
    update = lax.dot_general(
        weights, value_block, (((2,), (0,)), ((0,), (1,))), preferred_element_type=jnp.float32
    )
    return (acc_out * correct[:, :, None] + update, new_max, new_sum)


def attend_piece(state_now, query_rows, query_pos, kv_piece, key_pos, score_scale):
    row_count = kv_piece.shape[1]
    block_rows = row_count
    while block_rows > 2048 and block_rows % 2 == 0:
        block_rows = block_rows // 2
    block_count = row_count // block_rows
    blocks = jnp.moveaxis(kv_piece.reshape(2, block_count, block_rows, kv_piece.shape[2]), 1, 0)
    positions = key_pos.reshape(block_count, block_rows)

    def one_block(state_inner, block_item):
        return (
            attend(state_inner, query_rows, query_pos, block_item[0], block_item[1], score_scale),
            None,
        )

    final_state, unused = lax.scan(one_block, state_now, (blocks, positions))
    return final_state


def routed(queries, new_kv, pool, block_table, span_order):
    cycle_size = lax.axis_size("ctx")
    my_index = lax.axis_index("ctx")
    per_group = QH // KVH
    queries_dev = queries.shape[0]
    kv_heads = new_kv.shape[2] // HD
    pool_dev = pool.shape[1]
    block_len = pool.shape[2]
    blocks_dev = block_table.shape[0] // cycle_size
    owner_table = block_table.reshape(cycle_size, blocks_dev)
    holder = owner_table // pool_dev
    local_id = owner_table - holder * pool_dev
    same_holder = holder[:, :, None] == holder[:, None, :]
    earlier = (
        jnp.arange(blocks_dev, dtype=jnp.int32)[:, None]
        < jnp.arange(blocks_dev, dtype=jnp.int32)[None, :]
    )
    rank_in_list = jnp.sum((same_holder & earlier[None, :, :]).astype(jnp.int32), axis=1)
    slot_match = (holder[:, None, :] == my_index) & (
        rank_in_list[:, None, :] == jnp.arange(CAP, dtype=jnp.int32)[None, :, None]
    )
    source = jnp.sum(jnp.where(slot_match, local_id[:, None, :], 0), axis=2)
    filled = jnp.any(slot_match, axis=2)
    picked = jnp.take(pool, source.reshape(-1), axis=1)
    picked = jnp.where(filled.reshape(1, -1, 1, 1), picked, jnp.zeros_like(picked))
    outgoing = picked.reshape(2, cycle_size, CAP, block_len, pool.shape[3])
    incoming = lax.all_to_all(outgoing, "ctx", split_axis=1, concat_axis=1, tiled=True)
    my_holder = lax.dynamic_index_in_dim(holder, my_index, 0, keepdims=False)
    my_rank = lax.dynamic_index_in_dim(rank_in_list, my_index, 0, keepdims=False)
    flat_slot = my_holder * CAP + my_rank
    arrived = incoming.reshape(2, cycle_size * CAP, block_len, pool.shape[3])
    prefix_kv = jnp.take(arrived, flat_slot, axis=1).reshape(
        2, blocks_dev * block_len, pool.shape[3]
    )
    resident = jnp.concatenate([prefix_kv, new_kv], axis=1)
    resident_rows = resident.shape[1]
    prefix_rows_dev = blocks_dev * block_len
    prefix_total = cycle_size * prefix_rows_dev
    score_scale = 1.0 / math.sqrt(HD)
    row_offsets = jnp.arange(queries_dev, dtype=jnp.int32)
    own_span = lookup(my_index[None], span_order)[0]
    own_pos = jnp.repeat(prefix_total + own_span * queries_dev + row_offsets, per_group)
    query_rows = (
        queries.reshape(queries_dev, kv_heads, per_group, HD)
        .transpose(1, 0, 2, 3)
        .reshape(kv_heads, queries_dev * per_group, HD)
    )
    grouped_rows = queries_dev * per_group
    start_state = (
        jnp.zeros((kv_heads, grouped_rows, HD), jnp.float32),
        jnp.full((kv_heads, grouped_rows), masked_score, jnp.float32),
        jnp.zeros((kv_heads, grouped_rows), jnp.float32),
    )
    kv_piece = lax.all_gather(resident, "ctx", axis=1, tiled=True)
    positions = key_positions(
        kv_piece.shape[1], resident_rows, prefix_rows_dev, span_order, queries_dev, prefix_total
    )
    final_state = attend_piece(start_state, query_rows, own_pos, kv_piece, positions, score_scale)
    out_sum, out_max, out_total = final_state
    result = out_sum / out_total[:, :, None]
    result = (
        result.reshape(kv_heads, queries_dev, per_group, HD)
        .transpose(1, 0, 2, 3)
        .reshape(queries_dev, kv_heads * per_group * HD)
    )
    return result.astype(jnp.bfloat16)


def context_kernel(
    n, kv_heads, per_group, splits,
    order_ref, queries_ref, new_ref, pool_ref, out_ref,
    span_ref,
    kv, qs, acc, row_max, part_out, part_stat, got_out, got_stat,
    order_sem, load_sem, query_sem, kv_send, kv_recv, ask_send, ask_recv,
    part_send, part_recv, stat_send, stat_recv,
):
    me = lax.axis_index("ctx")
    at_edge = (me == 0) | (me == n - 1)
    inner = jnp.logical_not(at_edge)
    mate = jnp.where(me % 2 == 0, me + 1, me - 1)
    across = n - 1 - me
    far = n - 1 - mate
    helper = jnp.where(at_edge, far, across)
    my_role = jnp.where(at_edge, 2, 1)
    pool_dev, block_len = pool_ref.shape[1], pool_ref.shape[2]
    pieces, group_blocks = kv.shape[1], kv.shape[3]
    keys = group_blocks * block_len
    rows = queries_ref.shape[0]
    tile_heads = 2 if per_group % 2 == 0 else 1
    tile_rows = tile_heads * rows
    tiles = per_group // tile_heads
    halves = part_out.shape[2]
    half_heads = per_group // halves
    unit = math.log2(math.e) / math.sqrt(HD)
    MESH = pl.DeviceIdType.MESH

    def asker_of(role):
        return jnp.where(role == 0, me, jnp.where(role == 1, across, far))

    loads = [[] for _ in range(pieces)]
    count = 0
    for piece in range(pieces):
        kv_head, split = divmod(piece, splits)
        columns = pl.ds(kv_head * HD, HD)
        first = split * group_blocks
        pool_blocks = min(group_blocks, pool_dev - first)
        for t in range(2):
            if pool_blocks > 0:
                loads[piece].append(
                    pltpu.make_async_copy(
                        pool_ref.at[t, pl.ds(first, pool_blocks), :, columns],
                        kv.at[0, piece, t, pl.ds(0, pool_blocks)],
                        load_sem.at[count],
                    )
                )
                count += 1
            if pool_blocks < group_blocks:
                loads[piece].append(
                    pltpu.make_async_copy(
                        new_ref.at[t, :, columns],
                        kv.at[0, piece, t, group_blocks - 1],
                        load_sem.at[count],
                    )
                )
                count += 1
    for piece in range(pieces):
        for load in loads[piece]:
            load.start()
    order_load = pltpu.make_async_copy(order_ref, span_ref, order_sem)
    order_load.start()
    query_loads = []
    for head in range(kv_heads):
        for member in range(per_group):
            query_loads.append(
                pltpu.make_async_copy(
                    queries_ref.at[:, pl.ds((head * per_group + member) * HD, HD)],
                    qs.at[0, head, member],
                    query_sem.at[head * per_group + member],
                )
            )
            query_loads[-1].start()

    barrier = pltpu.get_barrier_semaphore()
    pl.semaphore_signal(barrier, inc=1, device_id={"ctx": mate}, device_id_type=MESH)
    pl.semaphore_signal(barrier, inc=1, device_id={"ctx": helper}, device_id_type=MESH)

    @pl.when(inner)
    def _():
        pl.semaphore_signal(barrier, inc=1, device_id={"ctx": far}, device_id_type=MESH)
        pl.semaphore_wait(barrier, 3)

    @pl.when(at_edge)
    def _():
        pl.semaphore_wait(barrier, 2)

    def kv_copy(piece):
        return pltpu.make_async_remote_copy(
            src_ref=kv.at[0, piece],
            dst_ref=kv.at[1, piece],
            send_sem=kv_send.at[piece],
            recv_sem=kv_recv.at[piece],
            device_id={"ctx": mate},
            device_id_type=MESH,
        )

    def ask_copy(head, role):
        return pltpu.make_async_remote_copy(
            src_ref=qs.at[0, head],
            dst_ref=qs.at[role, head],
            send_sem=ask_send.at[head],
            recv_sem=ask_recv.at[role - 1, head],
            device_id={"ctx": helper},
            device_id_type=MESH,
        )

    def part_copies(role, head, half):
        target = jnp.where(role == 1, across, far)
        return (
            pltpu.make_async_remote_copy(
                src_ref=part_out.at[role - 1, head, half],
                dst_ref=got_out.at[head, half],
                send_sem=part_send.at[role - 1, head, half],
                recv_sem=part_recv.at[head, half],
                device_id={"ctx": target},
                device_id_type=MESH,
            ),
            pltpu.make_async_remote_copy(
                src_ref=part_stat.at[role - 1, head, half],
                dst_ref=got_stat.at[head, half],
                send_sem=stat_send.at[role - 1, head, half],
                recv_sem=stat_recv.at[head, half],
                device_id={"ctx": target},
                device_id_type=MESH,
            ),
        )

    last_head = kv_heads - 1
    held_back = last_head * splits

    def ask_all():
        for head in range(kv_heads):
            for load in query_loads[head * per_group : (head + 1) * per_group]:
                load.wait()
            ask_copy(head, my_role).start()

    @pl.when(inner)
    def _():
        ask_all()

    for piece in range(pieces):
        for load in loads[piece]:
            load.wait()
        if piece < held_back:
            kv_copy(piece).start()

    @pl.when(at_edge)
    def _():
        ask_all()

    @pl.when(inner)
    def _():
        for piece in range(held_back, pieces):
            kv_copy(piece).start()

    query_row = lax.broadcasted_iota(jnp.int32, (tile_heads, rows, block_len), 1).reshape(
        tile_rows, block_len
    )
    key_column = lax.broadcasted_iota(jnp.int32, (tile_rows, block_len), 1)
    offset = key_column - query_row

    def attend_tiles(role, head, slot, split, count, fresh=False, half=None):
        taken = pl.ds(head * splits + split, count)
        width = count * keys
        key_rows = kv[slot, taken, 0].reshape(width, HD)
        value_rows = kv[slot, taken, 1].reshape(width, HD)
        value_ones = jnp.concatenate([value_rows, jnp.ones_like(value_rows)], axis=1)
        limit = (span_ref[asker_of(role)] - span_ref[jnp.where(slot == 0, me, mate)]) * rows
        if count < splits:
            has_new = split == splits - 1
            limit = jnp.where(has_new, limit, rows + block_len)
        allowed = offset <= limit
        first_row = 0 if half is None else pl.multiple_of(half * (half_heads * rows), tile_rows)
        first_head = 0 if half is None else half * half_heads
        for tile in range(tiles if half is None else tiles // halves):
            heads = pl.ds(first_head + tile * tile_heads, tile_heads)
            query_tile = qs[role, head, heads].reshape(tile_rows, HD)
            scores = lax.dot_general(
                query_tile, key_rows, (((1,), (1,)), ((), ())), preferred_element_type=jnp.float32
            )
            last = jnp.where(allowed, scores[:, width - block_len :], masked_score)
            scores = jnp.concatenate([scores[:, : width - block_len], last], axis=1)
            span = pl.ds(first_row + tile * tile_rows, tile_rows)
            new_max = jnp.max(scores, axis=1, keepdims=True)
            if fresh:
                new_max = jnp.broadcast_to(new_max, (tile_rows, HD))
            else:
                old_max = row_max[role, head, span]
                new_max = jnp.maximum(old_max, new_max)
            row_max[role, head, span] = new_max
            wide = jnp.concatenate([new_max] * (width // HD), axis=1)
            weights = jnp.exp2((scores - wide) * unit).astype(jnp.bfloat16)
            update = jnp.dot(weights, value_ones, preferred_element_type=jnp.float32)
            if not fresh:
                correct = jnp.exp2((old_max - new_max) * unit)
                update += acc[role, head, span] * jnp.concatenate([correct, correct], axis=1)
            acc[role, head, span] = update

    diagonal = lax.broadcasted_iota(jnp.int32, (rows, HD), 0) == lax.broadcasted_iota(
        jnp.int32, (rows, HD), 1
    )

    def return_part(role, head, half):
        for member in range(half_heads):
            first = (half * half_heads + member) * rows
            span = pl.ds(pl.multiple_of(first, rows), rows)
            total = acc[role, head, span, HD:]
            part_out[role - 1, head, half, member] = (acc[role, head, span, :HD] / total).astype(
                jnp.bfloat16
            )
            peak = row_max[role, head, span]
            part_stat[role - 1, head, half, pl.ds(member, 1)] = jnp.sum(
                jnp.where(diagonal, peak, 0.0), axis=0, keepdims=True
            )
            part_stat[role - 1, head, half, pl.ds(half_heads + member, 1)] = jnp.sum(
                jnp.where(diagonal, total, 0.0), axis=0, keepdims=True
            )
        for copy in part_copies(role, head, half):
            copy.start()

    order_load.wait()

    def near_keys(step, carry):
        role, head = step // kv_heads, step % kv_heads

        @pl.when((role == 0) | inner)
        def _():
            @pl.when(role == 1)
            def _():
                ask_copy(head, 1).wait_recv()

            attend_tiles(role, head, 0, 0, splits, fresh=True)

        return carry

    lax.fori_loop(0, 2 * kv_heads, near_keys, 0)

    @pl.when(at_edge)
    def _():
        for piece in range(held_back):
            kv_copy(piece).wait_send()
        for piece in range(held_back, pieces):
            kv_copy(piece).start()

    for head in range(last_head):
        for split in range(splits):
            kv_copy(head * splits + split).wait_recv()

        def one_role(step, carry, head=head):
            role = (step + 1) % 3

            @pl.when((role == 0) | inner)
            def _():
                @pl.when(role == 2)
                def _():
                    ask_copy(head, 2).wait_recv()
                    attend_tiles(role, head, 0, 0, splits, fresh=True)

                attend_tiles(role, head, 1, 0, splits)

                @pl.when(role > 0)
                def _():
                    def one_half(half, carry):
                        return_part(role, head, half)
                        return carry

                    lax.fori_loop(0, halves, one_half, 0)

            return carry

        lax.fori_loop(0, 3, one_role, 0)

    @pl.when(inner)
    def _():
        ask_copy(last_head, 2).wait_recv()
        attend_tiles(2, last_head, 0, 0, splits, fresh=True)

    def last_pieces(step, carry):
        split, role = step // 3, (step + 1) % 3

        @pl.when(role == 1)
        def _():
            kv_copy(held_back + split).wait_recv()

        @pl.when((role == 0) | inner)
        def _():
            def one_half(half, carry):
                attend_tiles(role, last_head, 1, split, 1, half=half)

                @pl.when((role > 0) & (split == splits - 1))
                def _():
                    return_part(role, last_head, half)

                return carry

            lax.fori_loop(0, halves, one_half, 0)

        return carry

    lax.fori_loop(0, 3 * splits, last_pieces, 0)

    def settle(head, half, member):
        index = half * half_heads + member
        span = pl.ds(index * rows, rows)
        their_max = jnp.broadcast_to(got_stat[head, half, pl.ds(member, 1)], (HD, rows)).T
        their_total = jnp.broadcast_to(
            got_stat[head, half, pl.ds(half_heads + member, 1)], (HD, rows)
        ).T
        my_max = row_max[0, head, span]
        top = jnp.maximum(my_max, their_max)
        mine = jnp.exp2((my_max - top) * unit)
        theirs = jnp.exp2((their_max - top) * unit) * their_total
        total = acc[0, head, span, HD:] * mine + theirs
        summed = acc[0, head, span, :HD] * mine + got_out[head, half, member].astype(jnp.float32) * theirs
        columns = pl.ds((head * per_group + index) * HD, HD)
        out_ref[:, columns] = (summed / total).astype(out_ref.dtype)

    for head in range(kv_heads):
        for half in range(halves):
            for copy in part_copies(my_role, head, half):
                copy.wait_recv()
            for member in range(half_heads):
                settle(head, half, member)

    @pl.when(inner)
    def _():
        for piece in range(held_back):
            kv_copy(piece).wait_send()
        for role in (1, 2):
            for head in range(kv_heads):
                for half in range(halves):
                    for copy in part_copies(role, head, half):
                        copy.wait_send()

    for piece in range(held_back, pieces):
        kv_copy(piece).wait_send()
    for head in range(kv_heads):
        ask_copy(head, my_role).wait_send()


def local(queries, new_kv, pool, block_table, span_order):
    n = lax.axis_size("ctx")
    pool_dev, block_len = pool.shape[1], pool.shape[2]
    rows = queries.shape[0]
    kv_heads = new_kv.shape[2] // HD
    per_group = QH // KVH
    whole_pool = block_table.shape[0] == n * pool_dev
    if not whole_pool or n != 4 or rows != block_len or rows != HD:
        return routed(queries, new_kv, pool, block_table, span_order)
    blocks = pool_dev + 1
    splits = 3 if blocks % 3 == 0 and blocks > 3 else 1
    pieces = kv_heads * splits
    group_blocks = blocks // splits
    group_rows = per_group * rows
    halves = 4 if per_group % 8 == 0 else 1
    work = queries.shape[1] * rows * block_len * blocks * n
    return pl.pallas_call(
        functools.partial(context_kernel, n, kv_heads, per_group, splits),
        out_shape=jax.ShapeDtypeStruct(queries.shape, jnp.bfloat16),
        in_specs=[
            pl.BlockSpec(memory_space=pltpu.HBM),
            pl.BlockSpec(memory_space=pltpu.HBM),
            pl.BlockSpec(memory_space=pltpu.HBM),
            pl.BlockSpec(memory_space=pltpu.HBM),
        ],
        out_specs=pl.BlockSpec(memory_space=pltpu.VMEM),
        scratch_shapes=[
            pltpu.SMEM(span_order.shape, jnp.int32),
            pltpu.VMEM((2, pieces, 2, group_blocks, block_len, HD), jnp.bfloat16),
            pltpu.VMEM((3, kv_heads, per_group, rows, HD), jnp.bfloat16),
            pltpu.VMEM((3, kv_heads, group_rows, 2 * HD), jnp.float32),
            pltpu.VMEM((3, kv_heads, group_rows, HD), jnp.float32),
            pltpu.VMEM((2, kv_heads, halves, per_group // halves, rows, HD), jnp.bfloat16),
            pltpu.VMEM((2, kv_heads, halves, 2 * (per_group // halves), HD), jnp.float32),
            pltpu.VMEM((kv_heads, halves, per_group // halves, rows, HD), jnp.bfloat16),
            pltpu.VMEM((kv_heads, halves, 2 * (per_group // halves), HD), jnp.float32),
            pltpu.SemaphoreType.DMA,
            pltpu.SemaphoreType.DMA((4 * pieces,)),
            pltpu.SemaphoreType.DMA((kv_heads * per_group,)),
            pltpu.SemaphoreType.DMA((pieces,)),
            pltpu.SemaphoreType.DMA((pieces,)),
            pltpu.SemaphoreType.DMA((kv_heads,)),
            pltpu.SemaphoreType.DMA((2, kv_heads)),
            pltpu.SemaphoreType.DMA((2, kv_heads, halves)),
            pltpu.SemaphoreType.DMA((kv_heads, halves)),
            pltpu.SemaphoreType.DMA((2, kv_heads, halves)),
            pltpu.SemaphoreType.DMA((kv_heads, halves)),
        ],
        compiler_params=pltpu.CompilerParams(
            collective_id=0, has_side_effects=True, vmem_limit_bytes=40 * 1024 * 1024
        ),
        cost_estimate=pl.CostEstimate(
            flops=4 * work, bytes_accessed=4 * queries.size, transcendentals=work // HD
        ),
        name="context_attention",
    )(
        *(
            pltpu.with_memory_space_constraint(held, pltpu.HBM)
            for held in (span_order, queries, new_kv, pool)
        )
    )


def solution(mesh):
    return jax.shard_map(
        local,
        mesh=mesh,
        in_specs=(
            P(("group", "ctx"), ("head", "pool")),
            P(None, ("group", "ctx"), ("head", "pool")),
            P(None, ("group", "ctx"), None, ("head", "pool")),
            P("group"),
            P("group"),
        ),
        out_specs=P(("group", "ctx"), ("head", "pool")),
        check_vma=False,
    )
```
